256 devices in a mesh: dp: 64 (over z, x, core), head: 4 (over y).
Axes of the slice: x: 4, y: 4, z: 8, core: 2. Of those that a mesh axis runs over, the one named last changes fastest.
Arguments:
- q_raw: bfloat16 [98304, 2560], P('dp', 'head'), may hold values from -2000 to 2000
- k_raw: bfloat16 [98304, 512], P('dp', 'head'), may hold values from -2000 to 2000
- v_proj: bfloat16 [98304, 512], P('dp', 'head'), may hold values from -6 to 6
- d_out: bfloat16 [98304, 2560], P('dp', 'head'), may hold values from -6 to 6
- q_gain: float32 [2560], P('head'), may hold values from 0.5 to 2
- k_gain: float32 [512], P('head'), may hold values from 0.5 to 2
- doc_lengths: int32 [64, 36], P('dp'), may hold values from 1 to 381, as said below
- plan_dest: int32 [64, 36], P('dp'), may hold values from 0 to 63, as said below
- plan_offset: int32 [64, 36], P('dp'), may hold values from 0 to 24, as said below
Outputs:
- grad_q: bfloat16 [98304, 2560], P('dp', 'head')
- grad_k: bfloat16 [98304, 512], P('dp', 'head')
- grad_v: bfloat16 [98304, 512], P('dp', 'head')
- balanced_lse: float32 [20, 221184], P('head', 'dp')
The draws below stay inside these ranges and needn't reach their ends.
Inputs may be any that keep to these rules, and one draw needn't show every extreme that they name: `doc_lengths`: each row holds the lengths of one sequence's documents in order and sums to 1536; the largest and the smallest length are reached in every draw. In each row exactly 32 documents have a plan_dest other than the row's own device, no two of them the same device; each of them has 24 to 48 rows, and in every row one has exactly 48 rows and one exactly 24. The documents that keep the row's own device sum to exactly 384 tokens. For a document sent to another device, plan_offset plus its length is at most 48; documents that stay have 0. Every row reaches the largest value.
All inputs are finite; a program needn't handle non-finite values.
Results may differ from the reference program's by a relative error of at most 0.008.
The reference program's roundings to bfloat16 on the way (of `q_norm`, `k_norm`, `weights_low`, `grad_scores`, `dq_norm` and `dk_norm`) count: a program that leaves them out, or rounds other values in their place, can miss the bound.
Values may be sent and summed in bfloat16 or wider, within the bound.
No kernel may reach another device: no remote copies, remote signals or barrier semaphores. Data moves between devices by JAX's collectives and lax.ppermute only.
A program may use at most 128 MiB of HBM per device.

```python
import math
from functools import partial
import jax
import jax.numpy as jnp
from jax import lax

HEADS = 20
KV_HEADS = 4
HDIM = 128
TOK_DEV = 1536
KEEP = 4
HOME = 384
SLOT = 48
MOVED = 32
DOCS = 36
TOKENS = 98304
QW = 2560
KW = 512
BALANCED = 221184
N_DP = 64


def plan_layout(key):
    chooser = jax.random.fold_in(key, 5)
    heavy = jax.random.permutation(chooser, N_DP) < N_DP // 4
    quarter = SLOT // 4
    half_pairs = MOVED // 2
    eighth = HOME // 8
    part_len = HOME // 4

    def one_source(index):
        inner = jax.random.fold_in(jax.random.fold_in(key, 9), index)
        streams = jax.random.split(inner, 5)
        spread = jax.random.randint(streams[0], (half_pairs,), 0, quarter + 1).astype(jnp.int32)
        spread = spread.at[0].set(quarter)
        moved_len = jnp.stack([3 * quarter + spread, 3 * quarter - spread], axis=1).reshape(MOVED).astype(jnp.int32)
        moved_shift = (jax.random.randint(streams[1], (MOVED,), 0, SLOT + 1) % (SLOT - moved_len + 1)).astype(jnp.int32)
        moved_shift = moved_shift.at[1].set(SLOT // 2)
        jitter = jax.random.randint(streams[2], (2,), 0, eighth + 1).astype(jnp.int32)
        light_len = jnp.stack([part_len + jitter[0], part_len - jitter[0], part_len + jitter[1], part_len - jitter[1]]).astype(jnp.int32)
        heavy_len = jnp.array([HOME - 3, 1, 1, 1], jnp.int32)
        keep_len = jnp.where(heavy[index], heavy_len, light_len).astype(jnp.int32)
        everyone = jnp.arange(N_DP, dtype=jnp.int32)
        avoid = (heavy & heavy[index]).astype(jnp.int32)
        ranking = jax.random.permutation(streams[3], N_DP).astype(jnp.int32) + N_DP * avoid + 2 * N_DP * (everyone == index).astype(jnp.int32)
        moved_dest = jnp.argsort(ranking)[:MOVED].astype(jnp.int32)
        lengths = jnp.concatenate([moved_len, keep_len])
        targets = jnp.concatenate([moved_dest, jnp.full((KEEP,), index, jnp.int32)])
        shifts = jnp.concatenate([moved_shift, jnp.zeros((KEEP,), jnp.int32)])
        order = jax.random.permutation(streams[4], DOCS)
        return (lengths[order], targets[order], shifts[order])
    return jax.vmap(one_source)(jnp.arange(N_DP, dtype=jnp.int32))


def draw_doc_lengths(key, part):
    layout = plan_layout(key)
    return layout[0]


def draw_plan_dest(key, part):
    layout = plan_layout(key)
    return layout[1]


def draw_plan_offset(key, part):
    layout = plan_layout(key)
    return layout[2]


def spread_scales(key, rows, width):
    first, second = jax.random.split(key)
    row_scale = jnp.exp(jax.random.uniform(first, (rows, 1), jnp.float32, 0.0, math.log(10.0)))
    rising = jnp.exp(jnp.arange(width, dtype=jnp.float32) * (math.log(3.0) / width))
    col_scale = jnp.exp(jax.random.uniform(second, (1, width), jnp.float32, 0.0, math.log(10.0))) * rising[None, :]
    return row_scale * col_scale


def draw_q_raw(key, part):
    key = jax.random.fold_in(key, 11)
    streams = jax.random.split(key, 2)
    width = HEADS * HDIM
    scales = spread_scales(streams[0], TOKENS, width)
    values = jnp.clip(jax.random.normal(streams[1], (TOKENS, width), jnp.float32), -6.0, 6.0) * scales
    return values.astype(jnp.bfloat16)


def draw_k_raw(key, part):
    key = jax.random.fold_in(key, 13)
    streams = jax.random.split(key, 2)
    width = KV_HEADS * HDIM
    scales = spread_scales(streams[0], TOKENS, width)
    values = jnp.clip(jax.random.normal(streams[1], (TOKENS, width), jnp.float32), -6.0, 6.0) * scales
    return values.astype(jnp.bfloat16)


def block_levels(rng, dims, cuts, low, high):
    loudness, own = 1.0, jax.random.fold_in(rng, 6)
    for axis_at, blocks in cuts:
        steps = jnp.exp(jax.random.uniform(jax.random.fold_in(own, axis_at), (blocks,), jnp.float32, low / len(cuts), high / len(cuts)))
        loudness = loudness * jnp.repeat(steps, dims[axis_at] // blocks).reshape([-1 if axis == axis_at else 1 for axis in range(len(dims))])
    return loudness


def bell_draw(rng, extent, scale, reach, cuts=(), kind=jnp.bfloat16):
    result = jax.random.normal(rng, extent, jnp.float32) * scale
    if len(cuts) > 0:
        result = block_levels(rng, extent, cuts, -0.22, 0.18) * result
    return jnp.clip(result, min=-reach, max=reach).astype(kind)


def setup_inputs(seed: int = 0) -> dict:
    key_of = jax.random.split(jax.random.key(seed), 10)
    q_raw = draw_q_raw(jax.random.fold_in(key_of[9], 71), 0)
    k_raw = draw_k_raw(jax.random.fold_in(key_of[9], 71), 0)
    v_proj = bell_draw(key_of[2], (TOKENS, KW), 1.0, 6.0, ((0, 64), (1, 4)))
    d_out = bell_draw(key_of[3], (TOKENS, QW), 1.0, 6.0, ((0, 64), (1, 4)))
    q_gain = jnp.clip(jnp.exp(math.log(2.0) - 1.3862944 * jax.random.uniform(key_of[4], (QW,), jnp.float32) ** block_levels(key_of[4], (QW,), ((0, 4),), -0.2, 0.2)), 0.5, 2.0)
    k_gain = jnp.clip(jnp.exp(math.log(2.0) - 1.3862944 * jax.random.uniform(key_of[5], (KW,), jnp.float32) ** block_levels(key_of[5], (KW,), ((0, 4),), -0.2, 0.2)), 0.5, 2.0)
    doc_lengths = draw_doc_lengths(jax.random.fold_in(key_of[9], 71), 0)
    plan_dest = draw_plan_dest(jax.random.fold_in(key_of[9], 71), 0)
    plan_offset = draw_plan_offset(jax.random.fold_in(key_of[9], 71), 0)
    return dict(q_raw=q_raw, k_raw=k_raw, v_proj=v_proj, d_out=d_out, q_gain=q_gain, k_gain=k_gain, doc_lengths=doc_lengths, plan_dest=plan_dest, plan_offset=plan_offset)


eps = 1e-06
big_negative = -1e+30

def rows_of_docs(doc_lengths):
    ends = jnp.cumsum(doc_lengths, axis=1).astype(jnp.int32)
    starts = (ends - doc_lengths).astype(jnp.int32)
    row_index = jnp.arange(TOK_DEV, dtype=jnp.int32)
    row_doc = lax.optimization_barrier(jnp.sum((row_index[None, :, None] >= ends[:, None, :]).astype(jnp.int32), axis=2)).astype(jnp.int32)
    return (starts, row_doc)

def one_sequence(inputs, q_gain, k_gain):
    q_raw, k_raw, v_proj, d_out, row_doc = inputs
    group_size = HEADS // KV_HEADS
    q_float = q_raw.astype(jnp.float32)
    k_float = k_raw.astype(jnp.float32)
    recip_q = lax.rsqrt(lax.optimization_barrier(jnp.mean(q_float * q_float, axis=1)) + eps)
    recip_k = lax.rsqrt(lax.optimization_barrier(jnp.mean(k_float * k_float, axis=1)) + eps)
    q_norm = lax.optimization_barrier((q_float * recip_q[:, None] * q_gain[None, :]).astype(jnp.bfloat16)).astype(jnp.float32)
    k_norm = lax.optimization_barrier((k_float * recip_k[:, None] * k_gain[None, :]).astype(jnp.bfloat16)).astype(jnp.float32)
    queries = q_norm.reshape(TOK_DEV, KV_HEADS, group_size, HDIM)
    key_heads = k_norm.reshape(TOK_DEV, KV_HEADS, HDIM)
    value_heads = v_proj.astype(jnp.float32).reshape(TOK_DEV, KV_HEADS, HDIM)
    upstream = d_out.astype(jnp.float32).reshape(TOK_DEV, KV_HEADS, group_size, HDIM)
    scaling = 1.0 / math.sqrt(HDIM)
    row_index = jnp.arange(TOK_DEV, dtype=jnp.int32)
    allowed = (row_doc[:, None] == row_doc[None, :]) & (row_index[None, :] <= row_index[:, None])
    scores = jnp.einsum('qgjd,kgd->gjqk', queries, key_heads) * scaling
    masked = jnp.where(allowed, scores, big_negative)
    row_peak = lax.optimization_barrier(jnp.max(masked, axis=-1, keepdims=True))
    row_total = lax.optimization_barrier(jnp.sum(jnp.where(allowed, jnp.exp(masked - row_peak), 0.0), axis=-1, keepdims=True))
    log_sums = row_peak + jnp.log(row_total)
    weights = jnp.where(allowed, jnp.exp(masked - log_sums), 0.0)
    weights_low = lax.optimization_barrier(weights.astype(jnp.bfloat16)).astype(jnp.float32)
    output = jnp.einsum('gjqk,kgd->qgjd', weights_low, value_heads)
    row_delta = jnp.transpose(lax.optimization_barrier(jnp.sum(upstream * output, axis=-1)), (1, 2, 0))[..., None]
    grad_values = jnp.einsum('gjqk,qgjd->kgd', weights_low, upstream)
    grad_weights = jnp.einsum('qgjd,kgd->gjqk', upstream, value_heads)
    grad_scores = weights * (grad_weights - row_delta) * scaling
    grad_low = lax.optimization_barrier(grad_scores.astype(jnp.bfloat16)).astype(jnp.float32)
    grad_query = jnp.einsum('gjqk,kgd->qgjd', grad_low, key_heads).reshape(TOK_DEV, -1)
    grad_keys = jnp.einsum('gjqk,qgjd->kgd', grad_low, queries).reshape(TOK_DEV, -1)
    dq_norm = lax.optimization_barrier(grad_query.astype(jnp.bfloat16)).astype(jnp.float32)
    dk_norm = lax.optimization_barrier(grad_keys.astype(jnp.bfloat16)).astype(jnp.float32)
    grad_v = grad_values.reshape(TOK_DEV, -1).astype(jnp.bfloat16)
    scaled_q = dq_norm * q_gain[None, :]
    back_q = lax.optimization_barrier(jnp.mean(scaled_q * q_float, axis=1))
    grad_q = (recip_q[:, None] * scaled_q - q_float * (recip_q ** 3 * back_q)[:, None]).astype(jnp.bfloat16)
    scaled_k = dk_norm * k_gain[None, :]
    back_k = lax.optimization_barrier(jnp.mean(scaled_k * k_float, axis=1))
    grad_k = (recip_k[:, None] * scaled_k - k_float * (recip_k ** 3 * back_k)[:, None]).astype(jnp.bfloat16)
    return (grad_q, grad_k, grad_v, log_sums[..., 0].reshape(HEADS, TOK_DEV))

def per_sequence(array):
    return array.reshape(N_DP, TOK_DEV, array.shape[1])

def reference(q_raw, k_raw, v_proj, d_out, q_gain, k_gain, doc_lengths, plan_dest, plan_offset):
    starts, row_doc = rows_of_docs(doc_lengths)
    worker = partial(one_sequence, q_gain=q_gain, k_gain=k_gain)
    grad_q, grad_k, grad_v, log_all = lax.map(worker, (per_sequence(q_raw), per_sequence(k_raw), per_sequence(v_proj), per_sequence(d_out), row_doc))
    row_dest = jnp.take_along_axis(plan_dest, row_doc, axis=1).astype(jnp.int32)
    row_start = jnp.take_along_axis(starts, row_doc, axis=1).astype(jnp.int32)
    row_shift = jnp.take_along_axis(plan_offset, row_doc, axis=1).astype(jnp.int32)
    source = jnp.arange(N_DP, dtype=jnp.int32)[:, None]
    position = jnp.arange(TOK_DEV, dtype=jnp.int32)[None, :]
    width_dev = HOME + 2 * TOK_DEV
    stay = row_dest == source
    rank = (jnp.cumsum(stay.astype(jnp.int32), axis=1) - 1).astype(jnp.int32)
    stay_column = source * width_dev + rank
    away_column = row_dest * width_dev + HOME + source * SLOT + row_shift + position - row_start
    target = jnp.where(stay, stay_column, away_column).astype(jnp.int32)
    flat = jnp.transpose(log_all, (1, 0, 2)).reshape(HEADS, TOKENS)
    balanced = jnp.zeros((HEADS, BALANCED), jnp.float32).at[:, target.reshape(-1)].set(flat)
    return (grad_q.reshape(TOKENS, -1), grad_k.reshape(TOKENS, -1), grad_v.reshape(TOKENS, -1), balanced)
```

```python
import functools
import math

import jax
import jax.numpy as jnp
from jax import lax
from jax.experimental import pallas as pl
from jax.experimental.pallas import tpu as pltpu
from jax.sharding import PartitionSpec as P

HDIM = 128
TILE = 128
SEQ = 1536
TILES = SEQ // TILE
GROUP = 5
DOCS = 36
DEVICES = 64
SLOT = 48
HOME = 384
REACH = 4
WIDTH_Q = 2560
WIDTH_K = 512

eps = 1e-06
big_negative = -1e30
scaling = 1.0 / math.sqrt(HDIM)
log2e = math.log2(math.e)
to_exp2 = scaling * log2e

f32 = jnp.float32
bf16 = jnp.bfloat16

VMEM = pl.BlockSpec(memory_space=pltpu.VMEM)
SMEM = pl.BlockSpec(memory_space=pltpu.SMEM)

mxu_nt = functools.partial(
    lax.dot_general, dimension_numbers=(((1,), (1,)), ((), ())), preferred_element_type=f32
)
mxu_nn = functools.partial(
    lax.dot_general, dimension_numbers=(((1,), (0,)), ((), ())), preferred_element_type=f32
)
mxu_tn = functools.partial(
    lax.dot_general, dimension_numbers=(((0,), (0,)), ((), ())), preferred_element_type=f32
)


def call(kernel, outs, ins, out_specs=None, scratch=(), flops=10**7, name=None):
    shapes = [jax.ShapeDtypeStruct(s, d) for s, d in outs]
    return pl.pallas_call(
        kernel,
        out_shape=shapes,
        in_specs=ins,
        out_specs=out_specs or [VMEM] * len(outs),
        scratch_shapes=list(scratch),
        compiler_params=pltpu.CompilerParams(vmem_limit_bytes=40 * 2**20),
        cost_estimate=pl.CostEstimate(flops=flops, bytes_accessed=10**6, transcendentals=0),
        name=name,
    )


def row_sums(values):
    return jnp.sum(jnp.transpose(values), axis=0, keepdims=True)


def fold(values):
    total = values[:, :HDIM]
    for h in range(1, values.shape[1] // HDIM):
        total = total + values[:, h * HDIM : (h + 1) * HDIM]
    return total


def square_kernel(q_ref, k_ref, out_ref):
    for i in range(TILES):
        rows = pl.ds(i * TILE, TILE)
        q = q_ref[rows, :].astype(f32)
        k = k_ref[rows, :].astype(f32)
        out_ref[i : i + 1, :] = row_sums(fold(q * q))
        out_ref[TILES + i : TILES + i + 1, :] = row_sums(k * k)


def layout_kernel(len_ref, start_ref, low_ref):
    rows = start_ref.shape[0]
    position = lax.broadcasted_iota(jnp.int32, (rows, TILE), 0) * TILE + lax.broadcasted_iota(
        jnp.int32, (rows, TILE), 1
    )
    zero = jnp.int32(0)

    def step(j, carry):
        end, start, lows = carry
        end = end + len_ref[0, j]
        start = jnp.where(position >= end, end, start)
        lows = tuple(jnp.where(end <= i * TILE, end, low) for i, low in enumerate(lows))
        return end, start, lows

    _, start, lows = lax.fori_loop(
        0, DOCS, step, (zero, jnp.zeros((rows, TILE), jnp.int32), (zero,) * TILES)
    )
    start_ref[...] = start
    for i in range(TILES):
        low_ref[i] = lows[i] // TILE


def columns_of(rows):
    stack = jnp.concatenate(rows + [jnp.zeros((8 - len(rows), TILE), f32)], axis=0)
    turned = jnp.transpose(stack)
    return [turned[:, j : j + 1] for j in range(len(rows))]


def allowed_of(start_row, low, tile, count):
    key = low * TILE + lax.broadcasted_iota(jnp.int32, (count * TILE, TILE), 0)
    query = tile * TILE + lax.broadcasted_iota(jnp.int32, (count * TILE, TILE), 1)
    return (key >= start_row) & (key <= query)


def forward_kernel(
    me_ref, low_ref, len_ref, dest_ref, shift_ref, start_ref,
    q_ref, k_ref, qg_ref, kg_ref, s0_ref, s1_ref, s2_ref, s3_ref,
    qn_ref, kn_ref, recip_ref, lse_ref, slot_ref, home_ref,
):
    total = s0_ref[...] + s1_ref[...] + s2_ref[...] + s3_ref[...]
    recip_ref[:TILES, :] = lax.rsqrt(total[:TILES] * (1.0 / WIDTH_Q) + eps)
    recip_ref[TILES:, :] = lax.rsqrt(total[TILES:] * (1.0 / WIDTH_K) + eps)
    slot_ref[...] = jnp.zeros(slot_ref.shape, f32)
    home_ref[...] = jnp.zeros(home_ref.shape, f32)
    lse_ref[TILES:] = jnp.zeros((lse_ref.shape[0] - TILES, 8, TILE), f32)

    def tile_step(i, carry):
        rows = pl.ds(pl.multiple_of(i * TILE, TILE), TILE)
        col_q, col_k = columns_of([recip_ref[pl.ds(i, 1), :], recip_ref[pl.ds(TILES + i, 1), :]])
        kn_ref[rows, :] = (k_ref[rows, :].astype(f32) * col_k * kg_ref[...]).astype(bf16)
        qn_ref[rows, :] = (q_ref[rows, :].astype(f32) * col_q * qg_ref[...]).astype(bf16)
        low = low_ref[i]
        count_here = i - low + 1
        start_row = start_ref[pl.ds(i, 1), :]

        for count in range(1, REACH + 1):

            @pl.when(count_here == count)
            def _(count=count):
                keys = kn_ref[pl.ds(pl.multiple_of(low * TILE, TILE), count * TILE), :]
                allowed = allowed_of(start_row, low, i, count)
                logs = []
                for h in range(GROUP):
                    raw = mxu_nt(keys, qn_ref[rows, h * HDIM : (h + 1) * HDIM])
                    masked = jnp.where(allowed, raw, big_negative)
                    peak = jnp.max(masked, axis=0, keepdims=True)
                    grown = jnp.exp2((masked - peak) * to_exp2)
                    logs.append(
                        peak * scaling + jnp.log(jnp.sum(grown, axis=0, keepdims=True))
                    )
                logs.append(jnp.zeros((8 - GROUP, TILE), f32))
                lse_ref[pl.ds(i, 1)] = jnp.concatenate(logs, axis=0)[None]

        return carry

    lax.fori_loop(0, TILES, tile_step, 0)

    me = me_ref[0]
    lane = lax.broadcasted_iota(jnp.int32, (8, TILE), 1)

    def doc_step(j, carry):
        start, kept = carry
        length = len_ref[0, j]
        dest = dest_ref[0, j]
        stays = dest == me

        @pl.when(jnp.logical_not(stays))
        def _():
            block = start // TILE
            inner = start % TILE
            place = (me * SLOT + shift_ref[0, j]) % TILE
            turn = (place - inner + TILE) % TILE
            here = pltpu.roll(lse_ref[block], turn, 1)
            after = pltpu.roll(lse_ref[block + 1], turn, 1)
            index = (lane - place) & (TILE - 1)
            value = jnp.where(index < TILE - inner, here, after)
            slot_ref[dest] = jnp.where(index < length, value, 0.0)

        @pl.when(stays)
        def _():
            gap = start - kept
            block = gap // TILE
            inner = gap % TILE
            turn = (TILE - inner) % TILE
            for b in range(HOME // TILE):
                here = pltpu.roll(lse_ref[block + b], turn, 1)
                after = pltpu.roll(lse_ref[block + b + 1], turn, 1)
                value = jnp.where(lane < TILE - inner, here, after)
                column = lane + b * TILE
                inside = (column >= kept) & (column < kept + length)
                part = slice(b * TILE, (b + 1) * TILE)
                home_ref[:, part] = jnp.where(inside, value, home_ref[:, part])

        return start + length, jnp.where(stays, kept + length, kept)

    lax.fori_loop(0, DOCS, doc_step, (jnp.int32(0), jnp.int32(0)))


def backward_kernel(
    low_ref, start_ref, qn_ref, kn_ref, v_ref, g_ref, lse_ref, q_ref, k_ref, qg_ref, kg_ref,
    dq_ref, dk_ref, dv_ref, sums_ref, dk_acc, dv_acc,
):
    dk_acc[...] = jnp.zeros(dk_acc.shape, f32)
    dv_acc[...] = jnp.zeros(dv_acc.shape, f32)

    def tile_step(i, carry):
        rows = pl.ds(pl.multiple_of(i * TILE, TILE), TILE)
        low = low_ref[i]
        count_here = i - low + 1
        start_row = start_ref[pl.ds(i, 1), :]

        for count in range(1, REACH + 1):

            @pl.when(count_here == count)
            def _(count=count):
                window = pl.ds(pl.multiple_of(low * TILE, TILE), count * TILE)
                keys = kn_ref[window, :]
                values = v_ref[window, :]
                allowed = allowed_of(start_row, low, i, count)
                logs = lse_ref[i] * log2e
                lows, grads, qs, gs = [], [], [], []
                for h in range(GROUP):
                    head = slice(h * HDIM, (h + 1) * HDIM)
                    q = qn_ref[rows, head]
                    g = g_ref[rows, head]
                    raw = mxu_nt(keys, q)
                    weights = jnp.where(
                        allowed, jnp.exp2(raw * to_exp2 - logs[h : h + 1, :]), 0.0
                    )
                    low_weights = weights.astype(bf16)
                    grad_weights = mxu_nt(values, g)
                    delta = jnp.sum(
                        low_weights.astype(f32) * grad_weights, axis=0, keepdims=True
                    )
                    grad = (weights * (grad_weights - delta) * scaling).astype(bf16)
                    lows.append(low_weights)
                    grads.append(grad)
                    qs.append(q)
                    gs.append(g)
                low_all = jnp.concatenate(lows, axis=1)
                grad_all = jnp.concatenate(grads, axis=1)
                dv_acc[window, :] += mxu_nn(low_all, jnp.concatenate(gs, axis=0))
                dk_acc[window, :] += mxu_nn(grad_all, jnp.concatenate(qs, axis=0))
                dq = mxu_tn(grad_all, keys).astype(bf16)
                for h in range(GROUP):
                    dq_ref[rows, h * HDIM : (h + 1) * HDIM] = dq[h * TILE : (h + 1) * TILE]

        scaled = dq_ref[rows, :].astype(f32) * qg_ref[...]
        sums_ref[pl.ds(i, 1), :] = row_sums(fold(scaled * q_ref[rows, :].astype(f32)))
        return carry

    lax.fori_loop(0, TILES, tile_step, 0)
    dk = dk_acc[...].astype(bf16)
    dk_ref[...] = dk
    dv_ref[...] = dv_acc[...].astype(bf16)
    scaled = dk.astype(f32) * kg_ref[...] * k_ref[...].astype(f32)
    for i in range(TILES):
        sums_ref[TILES + i : TILES + i + 1, :] = row_sums(scaled[i * TILE : (i + 1) * TILE])


def norm_kernel(
    q_ref, k_ref, dq_ref, dk_ref, qg_ref, kg_ref, recip_ref, s0_ref, s1_ref, s2_ref, s3_ref,
    gq_ref, gk_ref,
):
    recip = recip_ref[...]
    cube = recip * recip * recip * (s0_ref[...] + s1_ref[...] + s2_ref[...] + s3_ref[...])
    for i in range(TILES):
        rows = pl.ds(i * TILE, TILE)
        at_q, at_k = slice(i, i + 1), slice(TILES + i, TILES + i + 1)
        r_q, c_q, r_k, c_k = columns_of(
            [
                recip[at_q],
                cube[at_q] * (1.0 / WIDTH_Q),
                recip[at_k],
                cube[at_k] * (1.0 / WIDTH_K),
            ]
        )
        scaled = dq_ref[rows, :].astype(f32) * qg_ref[...]
        gq_ref[rows, :] = (r_q * scaled - q_ref[rows, :].astype(f32) * c_q).astype(bf16)
        scaled = dk_ref[rows, :].astype(f32) * kg_ref[...]
        gk_ref[rows, :] = (r_k * scaled - k_ref[rows, :].astype(f32) * c_k).astype(bf16)


def assemble_kernel(got_ref, home_ref, out_ref):
    out_ref[:, :HOME] = home_ref[:GROUP, :]
    lane = lax.broadcasted_iota(jnp.int32, (8, TILE), 1)
    for b in range(DEVICES * SLOT // TILE):
        total = None
        for s in range(b * TILE // SLOT, (b * TILE + TILE - 1) // SLOT + 1):
            left = s * SLOT - b * TILE
            value = got_ref[s]
            if left < 0:
                value = jnp.where(lane < left + SLOT, value, 0.0)
            if left + SLOT > TILE:
                value = jnp.where(lane >= left, value, 0.0)
            total = value if total is None else total + value
        out_ref[:, HOME + b * TILE : HOME + (b + 1) * TILE] = total[:GROUP]


def from_others(values):
    size = lax.axis_size("head")
    return [values] + [
        lax.ppermute(values, "head", [(i, (i + s) % size) for i in range(size)])
        for s in range(1, size)
    ]


def local(q_raw, k_raw, v_proj, d_out, q_gain, k_gain, doc_lengths, plan_dest, plan_offset):
    me = lax.axis_index("dp").astype(jnp.int32).reshape(1)
    qg = q_gain.reshape(1, -1)
    kg = k_gain.reshape(1, -1)
    stat = ((2 * TILES, TILE), f32)
    wide = ((SEQ, GROUP * HDIM), bf16)
    thin = ((SEQ, HDIM), bf16)

    (squares,) = call(square_kernel, [stat], [VMEM] * 2, name="squares")(q_raw, k_raw)
    start, low = call(
        layout_kernel,
        [((16, TILE), jnp.int32), ((TILES,), jnp.int32)],
        [SMEM],
        [VMEM, SMEM],
        name="layout",
    )(doc_lengths)
    qn, kn, recip, lse, slots, home = call(
        forward_kernel,
        [
            wide,
            thin,
            stat,
            ((16, 8, TILE), f32),
            ((DEVICES, 8, TILE), f32),
            ((8, HOME), f32),
        ],
        [SMEM] * 5 + [VMEM] * 9,
        name="forward",
    )(
        me, low, doc_lengths, plan_dest, plan_offset, start,
        q_raw, k_raw, qg, kg, *from_others(squares),
    )
    got = lax.all_to_all(slots, "dp", split_axis=0, concat_axis=0, tiled=True)
    dq, dk, grad_v, sums = call(
        backward_kernel,
        [wide, thin, thin, stat],
        [SMEM] + [VMEM] * 10,
        scratch=[pltpu.VMEM((SEQ, HDIM), f32)] * 2,
        flops=10**10,
        name="backward",
    )(low, start, qn, kn, v_proj, d_out, lse, q_raw, k_raw, qg, kg)
    grad_q, grad_k = call(norm_kernel, [wide, thin], [VMEM] * 11, name="normback")(
        q_raw, k_raw, dq, dk, qg, kg, recip, *from_others(sums)
    )
    (balanced,) = call(
        assemble_kernel, [((GROUP, HOME + DEVICES * SLOT), f32)], [VMEM] * 2, name="assemble"
    )(got, home)
    return grad_q, grad_k, grad_v, balanced


def solution(mesh):
    in_specs = (
        P("dp", "head"),
        P("dp", "head"),
        P("dp", "head"),
        P("dp", "head"),
        P("head"),
        P("head"),
        P("dp", None),
        P("dp", None),
        P("dp", None),
    )
    out_specs = (P("dp", "head"), P("dp", "head"), P("dp", "head"), P("head", "dp"))
    return jax.shard_map(local, mesh=mesh, in_specs=in_specs, out_specs=out_specs, check_vma=False)
```

```python
import functools
import math

import jax
import jax.numpy as jnp
from jax import lax
from jax.experimental import pallas as pl
from jax.experimental.pallas import tpu as pltpu
from jax.sharding import PartitionSpec as P

HDIM = 128
TILE = 128
SEQ = 1536
TILES = SEQ // TILE
GROUP = 5
DOCS = 36
DEVICES = 64
SLOT = 48
HOME = 384
STAYING = 4
WINDOWS = (128, 160, 192, 256, 384, 512)
KEPT_ROWS = TILES * 192 + 576
FAR_ROWS = 40000
WIDTH_Q = 2560
WIDTH_K = 512

eps = 1e-06
big_negative = -1e30
scaling = 1.0 / math.sqrt(HDIM)
log2e = math.log2(math.e)
to_exp2 = scaling * log2e

f32 = jnp.float32
bf16 = jnp.bfloat16

VMEM = pl.BlockSpec(memory_space=pltpu.VMEM)
SMEM = pl.BlockSpec(memory_space=pltpu.SMEM)
HBM = pl.BlockSpec(memory_space=pltpu.HBM)

mxu_nt = functools.partial(
    lax.dot_general, dimension_numbers=(((1,), (1,)), ((), ())), preferred_element_type=f32
)
mxu_nn = functools.partial(
    lax.dot_general, dimension_numbers=(((1,), (0,)), ((), ())), preferred_element_type=f32
)
mxu_tn = functools.partial(
    lax.dot_general, dimension_numbers=(((0,), (0,)), ((), ())), preferred_element_type=f32
)


def call(kernel, outs, ins, out_specs=None, scratch=(), flops=10**7, vmem=8, name=None):
    shapes = [jax.ShapeDtypeStruct(s, d) for s, d in outs]
    return pl.pallas_call(
        kernel,
        out_shape=shapes,
        in_specs=ins,
        out_specs=out_specs or [VMEM] * len(outs),
        scratch_shapes=list(scratch),
        compiler_params=pltpu.CompilerParams(vmem_limit_bytes=int(vmem * 2**20)),
        cost_estimate=pl.CostEstimate(flops=flops, bytes_accessed=10**6, transcendentals=0),
        name=name,
    )


def row_sums(values):
    return jnp.sum(jnp.transpose(values), axis=0, keepdims=True)


def column(row):
    return jnp.transpose(jnp.broadcast_to(row, (TILE, TILE)))


def spread(values):
    return jnp.concatenate([values] * GROUP, axis=1)


def fold(values):
    total = values[:, :HDIM]
    for h in range(1, values.shape[1] // HDIM):
        total = total + values[:, h * HDIM : (h + 1) * HDIM]
    return total


def turned(rows):
    return jnp.transpose(jnp.concatenate([rows, jnp.zeros((TILE - 2 * TILES, TILE), f32)], axis=0))


CHUNKS = 4
CHUNK = SEQ // CHUNKS


def square_kernel(q_ref, k_ref, out_ref, q_buf, k_buf, sems):
    copies = []
    for c in range(CHUNKS):
        rows = pl.ds(c * CHUNK, CHUNK)
        copies.append(pltpu.make_async_copy(q_ref.at[rows], q_buf.at[rows], sems.at[c]))
    copies.append(pltpu.make_async_copy(k_ref, k_buf, sems.at[CHUNKS]))
    copies[CHUNKS].start()
    for copy in copies[:CHUNKS]:
        copy.start()
    copies[CHUNKS].wait()
    for i in range(TILES):
        k = k_buf[i * TILE : (i + 1) * TILE, :].astype(f32)
        out_ref[TILES + i : TILES + i + 1, :] = row_sums(k * k)
    for i in range(TILES):
        if i % (TILES // CHUNKS) == 0:
            copies[i // (TILES // CHUNKS)].wait()
        q = q_buf[i * TILE : (i + 1) * TILE, :].astype(f32)
        out_ref[i : i + 1, :] = row_sums(fold(q * q))


def layout_kernel(me_ref, len_ref, dest_ref, start_ref, tile_ref, doc_ref, stay_ref):
    rows = start_ref.shape[0]
    position = lax.broadcasted_iota(jnp.int32, (rows, TILE), 0) * TILE + lax.broadcasted_iota(
        jnp.int32, (rows, TILE), 1
    )
    zero = jnp.int32(0)
    me = me_ref[0]

    def step(j, carry):
        end, start, kept, count, lows = carry
        length = len_ref[0, j]
        stays = dest_ref[0, j] == me
        doc_ref[j] = end
        slot = jnp.where(stays, jnp.minimum(count, STAYING - 1), STAYING)
        stay_ref[slot] = end
        stay_ref[8 + slot] = kept
        stay_ref[16 + slot] = length
        kept = jnp.where(stays, kept + length, kept)
        count = jnp.where(stays, count + 1, count)
        end = end + length
        start = jnp.where(position >= end, end, start)
        lows = tuple(jnp.where(end <= i * TILE, end, low) for i, low in enumerate(lows))
        return end, start, kept, count, lows

    _, start, _, _, lows = lax.fori_loop(
        0,
        DOCS,
        step,
        (zero, jnp.zeros((rows, TILE), jnp.int32), zero, zero, (zero,) * TILES),
    )
    start_ref[...] = start
    base = zero
    for i in range(TILES):
        need = (i + 1) * TILE - lows[i]
        size = jnp.int32(WINDOWS[0])
        for smaller, larger in zip(WINDOWS, WINDOWS[1:]):
            size = jnp.where(need > smaller, larger, size)
        tile_ref[i] = (i + 1) * TILE - size
        tile_ref[16 + i] = size
        tile_ref[32 + i] = base
        base = base + size


def window_of(tile_ref, i, size):
    return pl.ds(pl.multiple_of(tile_ref[i], 32), size), pl.ds(
        pl.multiple_of(tile_ref[32 + i], 32), size
    )


def kept_at(tile_ref, i, size, part):
    return pl.ds(pl.multiple_of(part * KEPT_ROWS + tile_ref[32 + i], 32), size)


def for_size(tile_ref, i, body):
    size_here = tile_ref[16 + i]
    for size in WINDOWS:

        @pl.when(size_here == size)
        def _(size=size):
            body(size)


def stacked(ref, rows):
    return jnp.concatenate([ref[rows, h * HDIM : (h + 1) * HDIM] for h in range(GROUP)], axis=0)


def scores_kernel(
    tile_ref, start_ref, q_hbm, k_hbm, v_hbm, g_hbm, qg_ref, kg_ref, s0_ref, s1_ref, s2_ref, s3_ref,
    kn_ref, recip_ref, lse_ref, kept_ref, dots_ref,
    dot_acc, qn_ref, q_ref, g_ref, k_ref, v_ref, buf_ref, in_sems, thin_sems, qn_sems, sems,
):
    per_chunk = TILES // CHUNKS

    def arrival(which, c):
        far, near = ((q_hbm, q_ref), (g_hbm, g_ref))[which]
        part = pl.ds(pl.multiple_of(c * CHUNK, CHUNK), CHUNK)
        return pltpu.make_async_copy(far.at[part], near.at[part], in_sems.at[which, c])

    k_copy = pltpu.make_async_copy(k_hbm, k_ref, thin_sems.at[0])
    v_copy = pltpu.make_async_copy(v_hbm, v_ref, thin_sems.at[1])
    k_copy.start()
    for c in range(CHUNKS):
        arrival(0, c).start()
    v_copy.start()
    for c in range(CHUNKS):
        arrival(1, c).start()
    total = s0_ref[...] + s1_ref[...] + s2_ref[...] + s3_ref[...]
    recip = jnp.concatenate(
        [
            lax.rsqrt(total[:TILES] * (1.0 / WIDTH_Q) + eps),
            lax.rsqrt(total[TILES:] * (1.0 / WIDTH_K) + eps),
        ],
        axis=0,
    )
    recip_ref[...] = recip
    columns = turned(recip)
    lse_ref[TILES:] = jnp.zeros((lse_ref.shape[0] - TILES, 8, TILE), f32)
    dot_acc[...] = jnp.zeros(dot_acc.shape, f32)
    k_copy.wait()
    for i in range(TILES):
        rows = slice(i * TILE, (i + 1) * TILE)
        col_k = columns[:, TILES + i : TILES + i + 1]
        kn_ref[rows, :] = (k_ref[rows, :].astype(f32) * col_k * kg_ref[...]).astype(bf16)

    def departure(c):
        near = pl.ds(pl.multiple_of(c * CHUNK, CHUNK), CHUNK)
        far = pl.ds(pl.multiple_of(2 * KEPT_ROWS + c * CHUNK, 32), CHUNK)
        return pltpu.make_async_copy(qn_ref.at[near], kept_ref.at[far], qn_sems.at[c])

    for i in range(TILES):
        if i % per_chunk == 0:
            arrival(0, i // per_chunk).wait()
        rows = slice(i * TILE, (i + 1) * TILE)
        col_q = columns[:, i : i + 1]
        qn_ref[rows, :] = (q_ref[rows, :].astype(f32) * col_q * qg_ref[...]).astype(bf16)
        if (i + 1) % per_chunk == 0:
            departure(i // per_chunk).start()
    v_copy.wait()

    def copies(i, size):
        return [
            pltpu.make_async_copy(
                buf_ref.at[kept_at(tile_ref, i, size, part)],
                kept_ref.at[kept_at(tile_ref, i, size, part)],
                sems.at[part, i],
            )
            for part in range(2)
        ]

    def tile_step(i, carry):
        rows = pl.ds(pl.multiple_of(i * TILE, TILE), TILE)
        start_row = start_ref[pl.ds(i, 1), :]

        @pl.when(lax.rem(i, per_chunk) == 0)
        def _():
            arrival(1, lax.div(i, per_chunk)).wait()

        def body(size):
            window = pl.ds(pl.multiple_of(tile_ref[i], 32), size)
            keys = kn_ref[window, :]
            values = v_ref[window, :]
            key = tile_ref[i] + lax.broadcasted_iota(jnp.int32, (size, TILE), 0)
            query = i * TILE + lax.broadcasted_iota(jnp.int32, (size, TILE), 1)
            bias = jnp.where((key >= start_row) & (key <= query), 0.0, big_negative)
            qs = stacked(qn_ref, rows)
            gs = stacked(g_ref, rows)
            masked = mxu_nt(keys, qs) + spread(bias)
            grad_weights = mxu_nt(values, gs)
            peak = jnp.max(masked, axis=0, keepdims=True)
            grown = jnp.exp2(masked * to_exp2 - peak * to_exp2)
            mass = jnp.sum(grown, axis=0, keepdims=True)
            logs = peak * scaling + jnp.log(mass)
            inverse = 1.0 / mass
            low = (grown * inverse).astype(bf16)
            buf_ref[kept_at(tile_ref, i, size, 0), :] = low
            delta = jnp.sum(low.astype(f32) * grad_weights, axis=0, keepdims=True)
            grad = grown * (inverse * scaling) * (grad_weights - delta)
            buf_ref[kept_at(tile_ref, i, size, 1), :] = grad.astype(bf16)
            dots = fold(grad * masked)
            logs = [logs[:, h * HDIM : (h + 1) * HDIM] for h in range(GROUP)]
            logs.append(jnp.zeros((8 - GROUP, TILE), f32))
            lse_ref[pl.ds(i, 1)] = jnp.concatenate(logs, axis=0)[None]
            dots_ref[pl.ds(i, 1), :] = jnp.sum(dots, axis=0, keepdims=True)
            dot_acc[window, :] += dots
            for copy in copies(i, size):
                copy.start()

        for_size(tile_ref, i, body)
        return carry

    lax.fori_loop(0, TILES, tile_step, 0)
    for i in range(TILES):
        dots_ref[TILES + i : TILES + i + 1, :] = row_sums(dot_acc[i * TILE : (i + 1) * TILE, :])
    for c in range(CHUNKS):
        departure(c).wait()

    def drain(i, carry):
        def body(size):
            for copy in copies(i, size):
                copy.wait()

        for_size(tile_ref, i, body)
        return carry

    lax.fori_loop(0, TILES, drain, 0)


def slot_kernel(
    me_ref, doc_ref, stay_ref, len_ref, dest_ref, shift_ref, lse_ref, slot_ref, home_ref, work
):
    me = me_ref[0]
    lane = lax.broadcasted_iota(jnp.int32, (8, TILE), 1)
    work[...] = jnp.zeros(work.shape, f32)
    for j in range(DOCS):
        dest = dest_ref[0, j]
        length = jnp.where(dest == me, 0, len_ref[0, j])
        block = doc_ref[j] >> 7
        inner = doc_ref[j] & (TILE - 1)
        place = shift_ref[0, j]
        turn = (place - inner) & (TILE - 1)
        here = pltpu.roll(lse_ref[block], turn, 1)
        after = pltpu.roll(lse_ref[block + 1], turn, 1)
        index = lane - place
        value = jnp.where(index < TILE - inner, here, after)
        work[dest] = jnp.where((index >= 0) & (index < length), value, 0.0)
    heads = [work[:, h, :] for h in range(GROUP)]
    wide = lax.broadcasted_iota(jnp.int32, (DEVICES, TILE), 1)
    gap_low = (wide >= 48) & (wide < 64)
    gap_high = wide >= 112
    last = heads[4]
    slot_ref[:, 0, :] = jnp.where(
        gap_low,
        pltpu.roll(last, 48, 1),
        jnp.where(gap_high, pltpu.roll(last, 96, 1), heads[0] + pltpu.roll(heads[1], 64, 1)),
    )
    slot_ref[:, 1, :] = jnp.where(
        gap_low, pltpu.roll(last, 16, 1), heads[2] + pltpu.roll(heads[3], 64, 1)
    )
    homes = [jnp.zeros((8, TILE), f32)] * (HOME // TILE)
    for n in range(STAYING):
        kept = stay_ref[8 + n]
        length = stay_ref[16 + n]
        gap = stay_ref[n] - kept
        block = gap >> 7
        inner = gap & (TILE - 1)
        turn = (TILE - inner) & (TILE - 1)
        moved = [pltpu.roll(lse_ref[block + b], turn, 1) for b in range(HOME // TILE + 1)]
        for b in range(HOME // TILE):
            value = jnp.where(lane < TILE - inner, moved[b], moved[b + 1])
            column = lane + b * TILE
            inside = (column >= kept) & (column < kept + length)
            homes[b] = jnp.where(inside, value, homes[b])
    home_ref[...] = jnp.concatenate(homes, axis=1)


def finish_kernel(
    tile_ref, kn_hbm, kept_ref, g_hbm, q_hbm, k_hbm, qg_ref, kg_ref, recip_ref,
    s0_ref, s1_ref, s2_ref, s3_ref,
    gq_ref, gk_ref, gv_ref,
    dk_acc, dv_acc, dq_buf, gq_buf, kn_ref, qn_ref, g_ref, q_ref, k_ref, gk_buf, gv_buf, buf_ref, cube_ref,
    in_sems, thin_sems, sems, out_sems,
):
    per_chunk = TILES // CHUNKS

    def chunk_copies(c):
        part = pl.ds(pl.multiple_of(c * CHUNK, CHUNK), CHUNK)
        far = pl.ds(pl.multiple_of(2 * KEPT_ROWS + c * CHUNK, 32), CHUNK)
        return [
            pltpu.make_async_copy(kept_ref.at[far], qn_ref.at[part], in_sems.at[0, c]),
            pltpu.make_async_copy(g_hbm.at[part], g_ref.at[part], in_sems.at[1, c]),
            pltpu.make_async_copy(q_hbm.at[part], q_ref.at[part], in_sems.at[2, c]),
        ]

    def out_copy(c):
        part = pl.ds(pl.multiple_of(c * CHUNK, CHUNK), CHUNK)
        return pltpu.make_async_copy(gq_buf.at[part], gq_ref.at[part], out_sems.at[c])

    def copies(i, size):
        return [
            pltpu.make_async_copy(
                kept_ref.at[kept_at(tile_ref, i, size, part)],
                buf_ref.at[kept_at(tile_ref, i, size, part)],
                sems.at[part, i],
            )
            for part in range(2)
        ]

    kn_copy = pltpu.make_async_copy(kn_hbm, kn_ref, thin_sems.at[0])
    k_copy = pltpu.make_async_copy(k_hbm, k_ref, thin_sems.at[1])
    gk_copy = pltpu.make_async_copy(gk_buf, gk_ref, thin_sems.at[2])
    gv_copy = pltpu.make_async_copy(gv_buf, gv_ref, thin_sems.at[3])
    kn_copy.start()

    def begin(i, carry):
        @pl.when(lax.rem(i, per_chunk) == 0)
        def _():
            for copy in chunk_copies(lax.div(i, per_chunk)):
                copy.start()

        def body(size):
            for copy in copies(i, size):
                copy.start()

        for_size(tile_ref, i, body)
        return carry

    lax.fori_loop(0, TILES, begin, 0)
    k_copy.start()
    dk_acc[...] = jnp.zeros(dk_acc.shape, f32)
    dv_acc[...] = jnp.zeros(dv_acc.shape, f32)
    recip = recip_ref[...]
    dots = s0_ref[...] + s1_ref[...] + s2_ref[...] + s3_ref[...]
    cube_ref[:TILES, :] = recip[:TILES] * recip[:TILES] * dots[:TILES] * (1.0 / WIDTH_Q)
    cube_ref[TILES:, :] = recip[TILES:] * recip[TILES:] * dots[TILES:] * (1.0 / WIDTH_K)
    kn_copy.wait()

    def finish_queries(i):
        rows = pl.ds(pl.multiple_of(i * TILE, TILE), TILE)
        factor = spread(column(recip_ref[pl.ds(i, 1), :])) * qg_ref[...]
        cube = spread(column(cube_ref[pl.ds(i, 1), :]))
        gq_buf[rows, :] = (
            factor * dq_buf[rows, :].astype(f32) - q_ref[rows, :].astype(f32) * cube
        ).astype(bf16)

    def tile_step(i, carry):
        rows = pl.ds(pl.multiple_of(i * TILE, TILE), TILE)

        @pl.when(lax.rem(i, per_chunk) == 0)
        def _():
            for copy in chunk_copies(lax.div(i, per_chunk)):
                copy.wait()

        def body(size):
            for copy in copies(i, size):
                copy.wait()
            finish_queries(jnp.maximum(i - 1, 0))
            window = pl.ds(pl.multiple_of(tile_ref[i], 32), size)
            weights = buf_ref[kept_at(tile_ref, i, size, 0), :]
            grads = buf_ref[kept_at(tile_ref, i, size, 1), :]
            dv_acc[window, :] += mxu_nn(weights, stacked(g_ref, rows))
            dk_acc[window, :] += mxu_nn(grads, stacked(qn_ref, rows))
            dq = mxu_tn(grads, kn_ref[window, :]).astype(bf16)
            for h in range(GROUP):
                dq_buf[rows, h * HDIM : (h + 1) * HDIM] = dq[h * TILE : (h + 1) * TILE]

        for_size(tile_ref, i, body)

        @pl.when((lax.rem(i, per_chunk) == 0) & (i > 0))
        def _():
            out_copy(lax.div(i, per_chunk) - 1).start()

        return carry

    dq_buf[:TILE, :] = jnp.zeros((TILE, GROUP * HDIM), bf16)
    lax.fori_loop(0, TILES, tile_step, 0)
    finish_queries(TILES - 1)
    out_copy(CHUNKS - 1).start()
    gv_buf[...] = dv_acc[...].astype(bf16)
    gv_copy.start()
    k_copy.wait()
    for i in range(TILES):
        rows = slice(i * TILE, (i + 1) * TILE)
        at = slice(TILES + i, TILES + i + 1)
        scaled = dk_acc[rows, :].astype(bf16).astype(f32) * kg_ref[...]
        gk_buf[rows, :] = (
            column(recip_ref[at, :]) * scaled - k_ref[rows, :].astype(f32) * column(cube_ref[at, :])
        ).astype(bf16)
    gk_copy.start()
    for c in range(CHUNKS):
        out_copy(c).wait()
    gv_copy.wait()
    gk_copy.wait()


def assemble_kernel(got_ref, home_ref, out_ref, work):
    out_ref[:, :HOME] = home_ref[:GROUP, :]
    upper, lower = got_ref[:, 0, :], got_ref[:, 1, :]
    wide = lax.broadcasted_iota(jnp.int32, (DEVICES, TILE), 1)
    work[:, 0, :] = upper
    work[:, 1, :] = pltpu.roll(upper, 64, 1)
    work[:, 2, :] = lower
    work[:, 3, :] = pltpu.roll(lower, 64, 1)
    work[:, 4, :] = jnp.where(
        wide < 16,
        pltpu.roll(upper, TILE - 48, 1),
        jnp.where(wide < 32, pltpu.roll(upper, TILE - 96, 1), pltpu.roll(lower, TILE - 16, 1)),
    )
    lane = lax.broadcasted_iota(jnp.int32, (8, TILE), 1)
    blocks = [None] * (DEVICES * SLOT // TILE)
    for s in range(DEVICES):
        block, place = divmod(s * SLOT, TILE)
        value = work[s]
        value = pltpu.roll(value, place, 1) if place else value
        if blocks[block] is None:
            blocks[block] = value
        else:
            blocks[block] = jnp.where(lane >= place, value, blocks[block])
        if place + SLOT > TILE:
            blocks[block + 1] = value
    for b, value in enumerate(blocks):
        out_ref[:, HOME + b * TILE : HOME + (b + 1) * TILE] = value[:GROUP]


def from_others(values):
    size = lax.axis_size("head")
    return [values] + [
        lax.ppermute(values, "head", [(i, (i + s) % size) for i in range(size)])
        for s in range(1, size)
    ]


def local(q_raw, k_raw, v_proj, d_out, q_gain, k_gain, doc_lengths, plan_dest, plan_offset):
    me = lax.axis_index("dp").astype(jnp.int32).reshape(1)
    qg = q_gain.reshape(1, -1)
    kg = k_gain.reshape(1, -1)
    stat = ((2 * TILES, TILE), f32)
    wide = ((SEQ, GROUP * HDIM), bf16)
    thin = ((SEQ, HDIM), bf16)
    logs = ((16, 8, TILE), f32)
    kept = ((FAR_ROWS, GROUP * HDIM), bf16)

    (squares,) = call(
        square_kernel,
        [stat],
        [HBM] * 2,
        scratch=[pltpu.VMEM(*wide), pltpu.VMEM(*thin), pltpu.SemaphoreType.DMA((CHUNKS + 1,))],
        vmem=53.7,
        name="squares",
    )(q_raw, k_raw)
    start, tiles, docs, stays = call(
        layout_kernel,
        [((16, TILE), jnp.int32), ((48,), jnp.int32), ((DOCS,), jnp.int32), ((24,), jnp.int32)],
        [SMEM] * 3,
        [VMEM] + [SMEM] * 3,
        name="layout",
    )(me, doc_lengths, plan_dest)
    kn, recip, lse, kept, dots = call(
        scores_kernel,
        [thin, stat, logs, kept, stat],
        [SMEM, VMEM] + [HBM] * 4 + [VMEM] * 6,
        out_specs=[VMEM] * 3 + [HBM, VMEM],
        scratch=[
            pltpu.VMEM((SEQ, HDIM), f32),
            pltpu.VMEM(*wide),
            pltpu.VMEM(*wide),
            pltpu.VMEM(*wide),
            pltpu.VMEM(*thin),
            pltpu.VMEM(*thin),
            pltpu.VMEM((2 * KEPT_ROWS, GROUP * HDIM), bf16),
            pltpu.SemaphoreType.DMA((2, CHUNKS)),
            pltpu.SemaphoreType.DMA((2,)),
            pltpu.SemaphoreType.DMA((CHUNKS,)),
            pltpu.SemaphoreType.DMA((2, TILES)),
        ],
        flops=10**9,
        vmem=53.7,
        name="scores",
    )(tiles, start, q_raw, k_raw, v_proj, d_out, qg, kg, *from_others(squares))
    all_dots = from_others(dots)
    slots, home = call(
        slot_kernel,
        [((DEVICES, 2, TILE), f32), ((8, HOME), f32)],
        [SMEM] * 6 + [VMEM],
        scratch=[pltpu.VMEM((DEVICES, 8, TILE), f32)],
        name="slots",
    )(me, docs, stays, doc_lengths, plan_dest, plan_offset, lse)
    got = lax.all_to_all(slots, "dp", split_axis=0, concat_axis=0, tiled=True)
    grad_q, grad_k, grad_v = call(
        finish_kernel,
        [wide, thin, thin],
        [SMEM] + [HBM] * 5 + [VMEM] * 7,
        out_specs=[HBM] * 3,
        scratch=[
            pltpu.VMEM((SEQ, HDIM), f32),
            pltpu.VMEM((SEQ, HDIM), f32),
            pltpu.VMEM(*wide),
            pltpu.VMEM(*wide),
            pltpu.VMEM(*thin),
            pltpu.VMEM(*wide),
            pltpu.VMEM(*wide),
            pltpu.VMEM(*wide),
            pltpu.VMEM(*thin),
            pltpu.VMEM(*thin),
            pltpu.VMEM(*thin),
            pltpu.VMEM((2 * KEPT_ROWS, GROUP * HDIM), bf16),
            pltpu.VMEM((2 * TILES, TILE), f32),
            pltpu.SemaphoreType.DMA((3, CHUNKS)),
            pltpu.SemaphoreType.DMA((4,)),
            pltpu.SemaphoreType.DMA((2, TILES)),
            pltpu.SemaphoreType.DMA((CHUNKS,)),
        ],
        flops=10**10,
        vmem=53.7,
        name="finish",
    )(tiles, kn, kept, d_out, q_raw, k_raw, qg, kg, recip, *all_dots)
    (balanced,) = call(
        assemble_kernel,
        [((GROUP, HOME + DEVICES * SLOT), f32)],
        [VMEM] * 2,
        scratch=[pltpu.VMEM((DEVICES, 8, TILE), f32)],
        name="assemble",
    )(got, home)
    return grad_q, grad_k, grad_v, balanced


def solution(mesh):
    in_specs = (
        P("dp", "head"),
        P("dp", "head"),
        P("dp", "head"),
        P("dp", "head"),
        P("head"),
        P("head"),
        P("dp", None),
        P("dp", None),
        P("dp", None),
    )
    out_specs = (P("dp", "head"), P("dp", "head"), P("dp", "head"), P("head", "dp"))
    return jax.shard_map(local, mesh=mesh, in_specs=in_specs, out_specs=out_specs, check_vma=False)
```

```python
import functools
import math

import jax
import jax.numpy as jnp
from jax import lax
from jax.experimental import pallas as pl
from jax.experimental.pallas import tpu as pltpu
from jax.sharding import PartitionSpec as P

HDIM = 128
TILE = 128
SEQ = 1536
TILES = SEQ // TILE
GROUP = 5
DOCS = 36
DEVICES = 64
SLOT = 48
HOME = 384
STAYING = 4
WINDOWS = (128, 160, 192, 256, 320, 384, 448, 512)
KEPT_ROWS = TILES * 192 + 576
FAR_ROWS = 40000
WIDTH_Q = 2560
WIDTH_K = 512

eps = 1e-06
big_negative = -1e30
scaling = 1.0 / math.sqrt(HDIM)
log2e = math.log2(math.e)
to_exp2 = scaling * log2e

f32 = jnp.float32
bf16 = jnp.bfloat16

KEYS_AT = pl.ds(2 * KEPT_ROWS + SEQ, SEQ)
VMEM = pl.BlockSpec(memory_space=pltpu.VMEM)
SMEM = pl.BlockSpec(memory_space=pltpu.SMEM)
HBM = pl.BlockSpec(memory_space=pltpu.HBM)

mxu_nt = functools.partial(
    lax.dot_general, dimension_numbers=(((1,), (1,)), ((), ())), preferred_element_type=f32
)
mxu_nn = functools.partial(
    lax.dot_general, dimension_numbers=(((1,), (0,)), ((), ())), preferred_element_type=f32
)
mxu_tn = functools.partial(
    lax.dot_general, dimension_numbers=(((0,), (0,)), ((), ())), preferred_element_type=f32
)


def call(kernel, outs, ins, out_specs=None, scratch=(), flops=10**7, vmem=8, name=None):
    shapes = [jax.ShapeDtypeStruct(s, d) for s, d in outs]
    return pl.pallas_call(
        kernel,
        out_shape=shapes,
        in_specs=ins,
        out_specs=out_specs or [VMEM] * len(outs),
        scratch_shapes=list(scratch),
        compiler_params=pltpu.CompilerParams(vmem_limit_bytes=int(vmem * 2**20)),
        cost_estimate=pl.CostEstimate(flops=flops, bytes_accessed=10**6, transcendentals=0),
        name=name,
    )


def row_sums(values):
    return jnp.sum(jnp.transpose(values), axis=0, keepdims=True)


def column(row):
    return jnp.transpose(jnp.broadcast_to(row, (TILE, TILE)))


def spread(values):
    return jnp.concatenate([values] * GROUP, axis=1)


def fold(values):
    total = values[:, :HDIM]
    for h in range(1, values.shape[1] // HDIM):
        total = total + values[:, h * HDIM : (h + 1) * HDIM]
    return total


def turned(rows):
    return jnp.transpose(jnp.concatenate([rows, jnp.zeros((TILE - 2 * TILES, TILE), f32)], axis=0))


CHUNKS = 4
CHUNK = SEQ // CHUNKS


def square_kernel(q_ref, k_ref, out_ref, q_buf, k_buf, sems):
    copies = []
    for c in range(CHUNKS):
        rows = pl.ds(c * CHUNK, CHUNK)
        copies.append(pltpu.make_async_copy(q_ref.at[rows], q_buf.at[rows], sems.at[c]))
    copies.append(pltpu.make_async_copy(k_ref, k_buf, sems.at[CHUNKS]))
    copies[CHUNKS].start()
    for copy in copies[:CHUNKS]:
        copy.start()
    copies[CHUNKS].wait()
    for i in range(TILES):
        k = k_buf[i * TILE : (i + 1) * TILE, :].astype(f32)
        out_ref[TILES + i : TILES + i + 1, :] = row_sums(k * k)
    for i in range(TILES):
        if i % (TILES // CHUNKS) == 0:
            copies[i // (TILES // CHUNKS)].wait()
        q = q_buf[i * TILE : (i + 1) * TILE, :].astype(f32)
        out_ref[i : i + 1, :] = row_sums(fold(q * q))


AT_DEST, AT_SENT, AT_PLACE, AT_STAY = DOCS, 2 * DOCS, 3 * DOCS, 4 * DOCS


def layout_kernel(
    me_ref, len_ref, dest_ref, shift_ref, q_far, k_far, v_far,
    start_ref, tile_ref, table_ref, q_near, k_near, v_near, sems,
):
    pairs = ((k_far, k_near), (v_far, v_near), (q_far, q_near))
    copies = [pltpu.make_async_copy(a, b, sems.at[n]) for n, (a, b) in enumerate(pairs)]
    for copy in copies:
        copy.start()
    rows = start_ref.shape[0]
    position = lax.broadcasted_iota(jnp.int32, (rows, TILE), 0) * TILE + lax.broadcasted_iota(
        jnp.int32, (rows, TILE), 1
    )
    zero = jnp.int32(0)
    me = me_ref[0]

    def step(j, carry):
        end, start, kept, count, lows = carry
        length = len_ref[0, j]
        stays = dest_ref[0, j] == me
        table_ref[j] = end
        table_ref[AT_DEST + j] = dest_ref[0, j]
        table_ref[AT_SENT + j] = jnp.where(stays, 0, length)
        table_ref[AT_PLACE + j] = shift_ref[0, j]
        slot = AT_STAY + jnp.where(stays, jnp.minimum(count, STAYING - 1), STAYING)
        table_ref[slot] = end
        table_ref[8 + slot] = kept
        table_ref[16 + slot] = length
        kept = jnp.where(stays, kept + length, kept)
        count = jnp.where(stays, count + 1, count)
        end = end + length
        start = jnp.where(position >= end, end, start)
        lows = tuple(jnp.where(end <= i * TILE, end, low) for i, low in enumerate(lows))
        return end, start, kept, count, lows

    _, start, _, _, lows = lax.fori_loop(
        0,
        DOCS,
        step,
        (zero, jnp.zeros((rows, TILE), jnp.int32), zero, zero, (zero,) * TILES),
        unroll=6,
    )
    start_ref[...] = start
    base = zero
    for i in range(TILES):
        need = (i + 1) * TILE - lows[i]
        size = jnp.int32(WINDOWS[0])
        for smaller, larger in zip(WINDOWS, WINDOWS[1:]):
            size = jnp.where(need > smaller, larger, size)
        tile_ref[i] = (i + 1) * TILE - size
        tile_ref[16 + i] = size
        tile_ref[32 + i] = base
        base = base + size
    for copy in copies:
        copy.wait()


def window_of(tile_ref, i, size):
    return pl.ds(pl.multiple_of(tile_ref[i], 32), size), pl.ds(
        pl.multiple_of(tile_ref[32 + i], 32), size
    )


def kept_at(tile_ref, i, size, part):
    return pl.ds(pl.multiple_of(part * KEPT_ROWS + tile_ref[32 + i], 32), size)


def for_size(tile_ref, i, body):
    size_here = tile_ref[16 + i]
    for size in WINDOWS:

        @pl.when(size_here == size)
        def _(size=size):
            body(size)


def fill_slots(table_ref, lse_ref, slot_ref, home_ref, work):
    lane = lax.broadcasted_iota(jnp.int32, (8, TILE), 1)
    work[...] = jnp.zeros(work.shape, f32)
    for j in range(DOCS):
        dest = table_ref[AT_DEST + j]
        length = table_ref[AT_SENT + j]
        block = table_ref[j] >> 7
        inner = table_ref[j] & (TILE - 1)
        place = table_ref[AT_PLACE + j]
        turn = (place - inner) & (TILE - 1)
        here = pltpu.roll(lse_ref[block], turn, 1)
        after = pltpu.roll(lse_ref[block + 1], turn, 1)
        index = lane - place
        value = jnp.where(index < TILE - inner, here, after)
        work[dest] = jnp.where((index >= 0) & (index < length), value, 0.0)
    heads = [work[:, h, :] for h in range(GROUP)]
    wide = lax.broadcasted_iota(jnp.int32, (DEVICES, TILE), 1)
    gap_low = (wide >= 48) & (wide < 64)
    gap_high = wide >= 112
    last = heads[4]
    slot_ref[:, 0, :] = jnp.where(
        gap_low,
        pltpu.roll(last, 48, 1),
        jnp.where(gap_high, pltpu.roll(last, 96, 1), heads[0] + pltpu.roll(heads[1], 64, 1)),
    )
    slot_ref[:, 1, :] = jnp.where(
        gap_low, pltpu.roll(last, 16, 1), heads[2] + pltpu.roll(heads[3], 64, 1)
    )
    homes = [jnp.zeros((8, TILE), f32)] * (HOME // TILE)
    for n in range(STAYING):
        kept = table_ref[AT_STAY + 8 + n]
        length = table_ref[AT_STAY + 16 + n]
        gap = table_ref[AT_STAY + n] - kept
        block = gap >> 7
        inner = gap & (TILE - 1)
        turn = (TILE - inner) & (TILE - 1)
        moved = [pltpu.roll(lse_ref[block + b], turn, 1) for b in range(HOME // TILE + 1)]
        for b in range(HOME // TILE):
            value = jnp.where(lane < TILE - inner, moved[b], moved[b + 1])
            column = lane + b * TILE
            inside = (column >= kept) & (column < kept + length)
            homes[b] = jnp.where(inside, value, homes[b])
    home_ref[...] = jnp.concatenate(homes, axis=1)


def stacked(ref, rows):
    return jnp.concatenate([ref[rows, h * HDIM : (h + 1) * HDIM] for h in range(GROUP)], axis=0)


def scores_kernel(
    tile_ref, table_ref, start_ref, q_ref, k_ref, v_ref, g_hbm, qg_ref, kg_ref, s0_ref, s1_ref, s2_ref, s3_ref,
    recip_ref, kept_ref, dots_ref, slot_hbm, home_ref,
    dot_acc, kn_ref, lse_ref, qn_ref, g_ref, buf_ref, work, slot_ref, in_sems, qn_sems, thin_sems, sems,
):
    per_chunk = TILES // CHUNKS

    def arrival(c):
        part = pl.ds(pl.multiple_of(c * CHUNK, CHUNK), CHUNK)
        return pltpu.make_async_copy(g_hbm.at[part], g_ref.at[part], in_sems.at[c])

    for c in range(CHUNKS):
        arrival(c).start()
    total = s0_ref[...] + s1_ref[...] + s2_ref[...] + s3_ref[...]
    recip = jnp.concatenate(
        [
            lax.rsqrt(total[:TILES] * (1.0 / WIDTH_Q) + eps),
            lax.rsqrt(total[TILES:] * (1.0 / WIDTH_K) + eps),
        ],
        axis=0,
    )
    recip_ref[...] = recip
    columns = turned(recip)
    lse_ref[TILES:] = jnp.zeros((lse_ref.shape[0] - TILES, 8, TILE), f32)
    dot_acc[...] = jnp.zeros(dot_acc.shape, f32)
    for i in range(TILES):
        rows = slice(i * TILE, (i + 1) * TILE)
        col_k = columns[:, TILES + i : TILES + i + 1]
        kn_ref[rows, :] = (k_ref[rows, :].astype(f32) * col_k * kg_ref[...]).astype(bf16)

    kn_copy = pltpu.make_async_copy(kn_ref, kept_ref.at[KEYS_AT, pl.ds(0, HDIM)], thin_sems.at[0])
    kn_copy.start()

    def departure(c):
        near = pl.ds(pl.multiple_of(c * CHUNK, CHUNK), CHUNK)
        far = pl.ds(pl.multiple_of(2 * KEPT_ROWS + c * CHUNK, 32), CHUNK)
        return pltpu.make_async_copy(qn_ref.at[near], kept_ref.at[far], qn_sems.at[c])

    for i in range(TILES):
        rows = slice(i * TILE, (i + 1) * TILE)
        col_q = columns[:, i : i + 1]
        qn_ref[rows, :] = (q_ref[rows, :].astype(f32) * col_q * qg_ref[...]).astype(bf16)
        if (i + 1) % per_chunk == 0:
            departure(i // per_chunk).start()
    def copies(i, size):
        return [
            pltpu.make_async_copy(
                buf_ref.at[kept_at(tile_ref, i, size, part)],
                kept_ref.at[kept_at(tile_ref, i, size, part)],
                sems.at[part, i],
            )
            for part in range(2)
        ]

    def tile_step(i, carry):
        rows = pl.ds(pl.multiple_of(i * TILE, TILE), TILE)
        start_row = start_ref[pl.ds(i, 1), :]

        @pl.when(lax.rem(i, per_chunk) == 0)
        def _():
            arrival(lax.div(i, per_chunk)).wait()

        def body(size):
            window = pl.ds(pl.multiple_of(tile_ref[i], 32), size)
            keys = kn_ref[window, :]
            values = v_ref[window, :]
            key = tile_ref[i] + lax.broadcasted_iota(jnp.int32, (size, TILE), 0)
            query = i * TILE + lax.broadcasted_iota(jnp.int32, (size, TILE), 1)
            bias = jnp.where((key >= start_row) & (key <= query), 0.0, big_negative)
            qs = stacked(qn_ref, rows)
            gs = stacked(g_ref, rows)
            masked = mxu_nt(keys, qs) + spread(bias)
            grad_weights = mxu_nt(values, gs)
            peak = jnp.max(masked, axis=0, keepdims=True)
            grown = jnp.exp2(masked * to_exp2 - peak * to_exp2)
            mass = jnp.sum(grown, axis=0, keepdims=True)
            logs = peak * scaling + jnp.log(mass)
            inverse = 1.0 / mass
            low = (grown * inverse).astype(bf16)
            buf_ref[kept_at(tile_ref, i, size, 0), :] = low
            delta = jnp.sum(low.astype(f32) * grad_weights, axis=0, keepdims=True)
            grad = grown * (inverse * scaling) * (grad_weights - delta)
            buf_ref[kept_at(tile_ref, i, size, 1), :] = grad.astype(bf16)
            dots = fold(grad * masked)
            logs = [logs[:, h * HDIM : (h + 1) * HDIM] for h in range(GROUP)]
            logs.append(jnp.zeros((8 - GROUP, TILE), f32))
            lse_ref[pl.ds(i, 1)] = jnp.concatenate(logs, axis=0)[None]
            dots_ref[pl.ds(i, 1), :] = jnp.sum(dots, axis=0, keepdims=True)
            dot_acc[window, :] += dots
            for copy in copies(i, size):
                copy.start()

        for_size(tile_ref, i, body)
        return carry

    lax.fori_loop(0, TILES, tile_step, 0)
    fill_slots(table_ref, lse_ref, slot_ref, home_ref, work)
    slot_copy = pltpu.make_async_copy(slot_ref, slot_hbm, thin_sems.at[1])
    slot_copy.start()
    for i in range(TILES):
        dots_ref[TILES + i : TILES + i + 1, :] = row_sums(dot_acc[i * TILE : (i + 1) * TILE, :])
    kn_copy.wait()
    for c in range(CHUNKS):
        departure(c).wait()

    def drain(i, carry):
        def body(size):
            for copy in copies(i, size):
                copy.wait()

        for_size(tile_ref, i, body)
        return carry

    lax.fori_loop(0, TILES, drain, 0)
    slot_copy.wait()


def finish_kernel(
    tile_ref, kept_ref, g_hbm, q_hbm, k_hbm, qg_ref, kg_ref, recip_ref,
    s0_ref, s1_ref, s2_ref, s3_ref,
    gq_ref, gk_ref, gv_ref,
    dk_acc, dv_acc, dq_buf, gq_buf, kn_ref, qn_ref, g_ref, q_ref, k_ref, gk_buf, gv_buf, buf_ref, cube_ref,
    in_sems, thin_sems, sems, out_sems,
):
    per_chunk = TILES // CHUNKS

    def chunk_copies(c):
        part = pl.ds(pl.multiple_of(c * CHUNK, CHUNK), CHUNK)
        far = pl.ds(pl.multiple_of(2 * KEPT_ROWS + c * CHUNK, 32), CHUNK)
        return [
            pltpu.make_async_copy(kept_ref.at[far], qn_ref.at[part], in_sems.at[0, c]),
            pltpu.make_async_copy(g_hbm.at[part], g_ref.at[part], in_sems.at[1, c]),
            pltpu.make_async_copy(q_hbm.at[part], q_ref.at[part], in_sems.at[2, c]),
        ]

    def out_copy(c):
        part = pl.ds(pl.multiple_of(c * CHUNK, CHUNK), CHUNK)
        return pltpu.make_async_copy(gq_buf.at[part], gq_ref.at[part], out_sems.at[c])

    def copies(i, size):
        return [
            pltpu.make_async_copy(
                kept_ref.at[kept_at(tile_ref, i, size, part)],
                buf_ref.at[kept_at(tile_ref, i, size, part)],
                sems.at[part, i],
            )
            for part in range(2)
        ]

    kn_copy = pltpu.make_async_copy(kept_ref.at[KEYS_AT, pl.ds(0, HDIM)], kn_ref, thin_sems.at[0])
    k_copy = pltpu.make_async_copy(k_hbm, k_ref, thin_sems.at[1])
    gk_copy = pltpu.make_async_copy(gk_buf, gk_ref, thin_sems.at[2])
    gv_copy = pltpu.make_async_copy(gv_buf, gv_ref, thin_sems.at[3])
    kn_copy.start()

    def begin(i, carry):
        @pl.when(lax.rem(i, per_chunk) == 0)
        def _():
            for copy in chunk_copies(lax.div(i, per_chunk)):
                copy.start()

        def body(size):
            for copy in copies(i, size):
                copy.start()

        for_size(tile_ref, i, body)
        return carry

    lax.fori_loop(0, TILES, begin, 0)
    k_copy.start()
    dk_acc[...] = jnp.zeros(dk_acc.shape, f32)
    dv_acc[...] = jnp.zeros(dv_acc.shape, f32)
    recip = recip_ref[...]
    dots = s0_ref[...] + s1_ref[...] + s2_ref[...] + s3_ref[...]
    cube_ref[:TILES, :] = recip[:TILES] * recip[:TILES] * dots[:TILES] * (1.0 / WIDTH_Q)
    cube_ref[TILES:, :] = recip[TILES:] * recip[TILES:] * dots[TILES:] * (1.0 / WIDTH_K)
    kn_copy.wait()

    def finish_queries(i):
        rows = pl.ds(pl.multiple_of(i * TILE, TILE), TILE)
        factor = spread(column(recip_ref[pl.ds(i, 1), :])) * qg_ref[...]
        cube = spread(column(cube_ref[pl.ds(i, 1), :]))
        gq_buf[rows, :] = (
            factor * dq_buf[rows, :].astype(f32) - q_ref[rows, :].astype(f32) * cube
        ).astype(bf16)

    def tile_step(i, carry):
        rows = pl.ds(pl.multiple_of(i * TILE, TILE), TILE)

        @pl.when(lax.rem(i, per_chunk) == 0)
        def _():
            for copy in chunk_copies(lax.div(i, per_chunk)):
                copy.wait()

        def body(size):
            for copy in copies(i, size):
                copy.wait()
            finish_queries(jnp.maximum(i - 1, 0))
            window = pl.ds(pl.multiple_of(tile_ref[i], 32), size)
            weights = buf_ref[kept_at(tile_ref, i, size, 0), :]
            grads = buf_ref[kept_at(tile_ref, i, size, 1), :]
            dv_acc[window, :] += mxu_nn(weights, stacked(g_ref, rows))
            dk_acc[window, :] += mxu_nn(grads, stacked(qn_ref, rows))
            dq = mxu_tn(grads, kn_ref[window, :]).astype(bf16)
            for h in range(GROUP):
                dq_buf[rows, h * HDIM : (h + 1) * HDIM] = dq[h * TILE : (h + 1) * TILE]

        for_size(tile_ref, i, body)

        @pl.when((lax.rem(i, per_chunk) == 0) & (i > 0))
        def _():
            out_copy(lax.div(i, per_chunk) - 1).start()

        return carry

    dq_buf[:TILE, :] = jnp.zeros((TILE, GROUP * HDIM), bf16)
    lax.fori_loop(0, TILES, tile_step, 0)
    finish_queries(TILES - 1)
    out_copy(CHUNKS - 1).start()
    gv_buf[...] = dv_acc[...].astype(bf16)
    gv_copy.start()
    k_copy.wait()
    for i in range(TILES):
        rows = slice(i * TILE, (i + 1) * TILE)
        at = slice(TILES + i, TILES + i + 1)
        scaled = dk_acc[rows, :].astype(bf16).astype(f32) * kg_ref[...]
        gk_buf[rows, :] = (
            column(recip_ref[at, :]) * scaled - k_ref[rows, :].astype(f32) * column(cube_ref[at, :])
        ).astype(bf16)
    gk_copy.start()
    for c in range(CHUNKS):
        out_copy(c).wait()
    gv_copy.wait()
    gk_copy.wait()


def assemble_kernel(got_ref, home_ref, out_ref, work):
    out_ref[:, :HOME] = home_ref[:GROUP, :]
    upper, lower = got_ref[:, 0, :], got_ref[:, 1, :]
    wide = lax.broadcasted_iota(jnp.int32, (DEVICES, TILE), 1)
    work[:, 0, :] = upper
    work[:, 1, :] = pltpu.roll(upper, 64, 1)
    work[:, 2, :] = lower
    work[:, 3, :] = pltpu.roll(lower, 64, 1)
    work[:, 4, :] = jnp.where(
        wide < 16,
        pltpu.roll(upper, TILE - 48, 1),
        jnp.where(wide < 32, pltpu.roll(upper, TILE - 96, 1), pltpu.roll(lower, TILE - 16, 1)),
    )
    lane = lax.broadcasted_iota(jnp.int32, (8, TILE), 1)
    blocks = [None] * (DEVICES * SLOT // TILE)
    for s in range(DEVICES):
        block, place = divmod(s * SLOT, TILE)
        value = work[s]
        value = pltpu.roll(value, place, 1) if place else value
        if blocks[block] is None:
            blocks[block] = value
        else:
            blocks[block] = jnp.where(lane >= place, value, blocks[block])
        if place + SLOT > TILE:
            blocks[block + 1] = value
    for b, value in enumerate(blocks):
        out_ref[:, HOME + b * TILE : HOME + (b + 1) * TILE] = value[:GROUP]


def from_others(values):
    size = lax.axis_size("head")
    return [values] + [
        lax.ppermute(values, "head", [(i, (i + s) % size) for i in range(size)])
        for s in range(1, size)
    ]


def local(q_raw, k_raw, v_proj, d_out, q_gain, k_gain, doc_lengths, plan_dest, plan_offset):
    me = lax.axis_index("dp").astype(jnp.int32).reshape(1)
    qg = q_gain.reshape(1, -1)
    kg = k_gain.reshape(1, -1)
    stat = ((2 * TILES, TILE), f32)
    wide = ((SEQ, GROUP * HDIM), bf16)
    thin = ((SEQ, HDIM), bf16)
    kept = ((FAR_ROWS, GROUP * HDIM), bf16)

    (squares,) = call(
        square_kernel,
        [stat],
        [HBM] * 2,
        scratch=[pltpu.VMEM(*wide), pltpu.VMEM(*thin), pltpu.SemaphoreType.DMA((CHUNKS + 1,))],
        vmem=53.7,
        name="squares",
    )(q_raw, k_raw)
    start, tiles, table, q_near, k_near, v_near = call(
        layout_kernel,
        [
            ((16, TILE), jnp.int32),
            ((48,), jnp.int32),
            ((AT_STAY + 24,), jnp.int32),
            wide,
            thin,
            thin,
        ],
        [SMEM] * 4 + [HBM] * 3,
        [VMEM] + [SMEM] * 2 + [HBM] * 3,
        scratch=[pltpu.SemaphoreType.DMA((3,))],
        vmem=50.5,
        name="layout",
    )(me, doc_lengths, plan_dest, plan_offset, q_raw, k_raw, v_proj)
    recip, kept, dots, slots, home = call(
        scores_kernel,
        [stat, kept, stat, ((DEVICES, 2, TILE), f32), ((8, HOME), f32)],
        [SMEM] * 2 + [VMEM] * 4 + [HBM] + [VMEM] * 6,
        out_specs=[VMEM, HBM, VMEM, HBM, VMEM],
        scratch=[
            pltpu.VMEM((SEQ, HDIM), f32),
            pltpu.VMEM(*thin),
            pltpu.VMEM((16, 8, TILE), f32),
            pltpu.VMEM(*wide),
            pltpu.VMEM(*wide),
            pltpu.VMEM((2 * KEPT_ROWS, GROUP * HDIM), bf16),
            pltpu.VMEM((DEVICES, 8, TILE), f32),
            pltpu.VMEM((DEVICES, 2, TILE), f32),
            pltpu.SemaphoreType.DMA((CHUNKS,)),
            pltpu.SemaphoreType.DMA((CHUNKS,)),
            pltpu.SemaphoreType.DMA((2,)),
            pltpu.SemaphoreType.DMA((2, TILES)),
        ],
        flops=10**9,
        vmem=50.5,
        name="scores",
    )(tiles, table, start, q_near, k_near, v_near, d_out, qg, kg, *from_others(squares))
    all_dots = from_others(dots)
    got = lax.all_to_all(slots, "dp", split_axis=0, concat_axis=0, tiled=True)
    grad_q, grad_k, grad_v = call(
        finish_kernel,
        [wide, thin, thin],
        [SMEM] + [HBM] * 4 + [VMEM] * 7,
        out_specs=[HBM] * 3,
        scratch=[
            pltpu.VMEM((SEQ, HDIM), f32),
            pltpu.VMEM((SEQ, HDIM), f32),
            pltpu.VMEM(*wide),
            pltpu.VMEM(*wide),
            pltpu.VMEM(*thin),
            pltpu.VMEM(*wide),
            pltpu.VMEM(*wide),
            pltpu.VMEM(*wide),
            pltpu.VMEM(*thin),
            pltpu.VMEM(*thin),
            pltpu.VMEM(*thin),
            pltpu.VMEM((2 * KEPT_ROWS, GROUP * HDIM), bf16),
            pltpu.VMEM((2 * TILES, TILE), f32),
            pltpu.SemaphoreType.DMA((3, CHUNKS)),
            pltpu.SemaphoreType.DMA((4,)),
            pltpu.SemaphoreType.DMA((2, TILES)),
            pltpu.SemaphoreType.DMA((CHUNKS,)),
        ],
        flops=10**10,
        vmem=53.7,
        name="finish",
    )(tiles, kept, d_out, q_raw, k_raw, qg, kg, recip, *all_dots)
    (balanced,) = call(
        assemble_kernel,
        [((GROUP, HOME + DEVICES * SLOT), f32)],
        [VMEM] * 2,
        scratch=[pltpu.VMEM((DEVICES, 8, TILE), f32)],
        name="assemble",
    )(got, home)
    return grad_q, grad_k, grad_v, balanced


def solution(mesh):
    in_specs = (
        P("dp", "head"),
        P("dp", "head"),
        P("dp", "head"),
        P("dp", "head"),
        P("head"),
        P("head"),
        P("dp", None),
        P("dp", None),
        P("dp", None),
    )
    out_specs = (P("dp", "head"), P("dp", "head"), P("dp", "head"), P("head", "dp"))
    return jax.shard_map(local, mesh=mesh, in_specs=in_specs, out_specs=out_specs, check_vma=False)
```

```python
import functools
import math

import jax
import jax.numpy as jnp
from jax import lax
from jax.experimental import pallas as pl
from jax.experimental.pallas import tpu as pltpu
from jax.sharding import PartitionSpec as P

HDIM = 128
TILE = 128
SEQ = 1536
TILES = SEQ // TILE
GROUP = 5
DOCS = 36
DEVICES = 64
SLOT = 48
HOME = 384
STAYING = 4
WINDOWS = (128, 160, 192, 256, 320, 384, 448, 512)
KEPT_ROWS = TILES * 192 + 576
FAR_ROWS = 40000
WIDTH_Q = 2560
WIDTH_K = 512

eps = 1e-06
big_negative = -1e30
scaling = 1.0 / math.sqrt(HDIM)
log2e = math.log2(math.e)
to_exp2 = scaling * log2e

f32 = jnp.float32
bf16 = jnp.bfloat16

KEYS_AT = pl.ds(2 * KEPT_ROWS + SEQ, SEQ)
VMEM = pl.BlockSpec(memory_space=pltpu.VMEM)
SMEM = pl.BlockSpec(memory_space=pltpu.SMEM)
HBM = pl.BlockSpec(memory_space=pltpu.HBM)

mxu_nt = functools.partial(
    lax.dot_general, dimension_numbers=(((1,), (1,)), ((), ())), preferred_element_type=f32
)
mxu_nn = functools.partial(
    lax.dot_general, dimension_numbers=(((1,), (0,)), ((), ())), preferred_element_type=f32
)
mxu_tn = functools.partial(
    lax.dot_general, dimension_numbers=(((0,), (0,)), ((), ())), preferred_element_type=f32
)


def call(kernel, outs, ins, out_specs=None, scratch=(), flops=10**7, vmem=8, name=None):
    shapes = [jax.ShapeDtypeStruct(s, d) for s, d in outs]
    return pl.pallas_call(
        kernel,
        out_shape=shapes,
        in_specs=ins,
        out_specs=out_specs or [VMEM] * len(outs),
        scratch_shapes=list(scratch),
        compiler_params=pltpu.CompilerParams(vmem_limit_bytes=int(vmem * 2**20)),
        cost_estimate=pl.CostEstimate(flops=flops, bytes_accessed=10**6, transcendentals=0),
        name=name,
    )


def row_sums(values):
    return jnp.sum(jnp.transpose(values), axis=0, keepdims=True)


def column(row):
    return jnp.transpose(jnp.broadcast_to(row, (TILE, TILE)))


def spread(values):
    return jnp.concatenate([values] * GROUP, axis=1)


def fold(values):
    total = values[:, :HDIM]
    for h in range(1, values.shape[1] // HDIM):
        total = total + values[:, h * HDIM : (h + 1) * HDIM]
    return total


def turned(rows):
    return jnp.transpose(jnp.concatenate([rows, jnp.zeros((TILE - 2 * TILES, TILE), f32)], axis=0))


CHUNKS = 4
CHUNK = SEQ // CHUNKS


def square_kernel(q_ref, k_ref, out_ref, q_buf, k_buf, sems):
    copies = []
    for c in range(CHUNKS):
        rows = pl.ds(c * CHUNK, CHUNK)
        copies.append(pltpu.make_async_copy(q_ref.at[rows], q_buf.at[rows], sems.at[c]))
    copies.append(pltpu.make_async_copy(k_ref, k_buf, sems.at[CHUNKS]))
    copies[CHUNKS].start()
    for copy in copies[:CHUNKS]:
        copy.start()
    copies[CHUNKS].wait()
    for i in range(TILES):
        k = k_buf[i * TILE : (i + 1) * TILE, :].astype(f32)
        out_ref[TILES + i : TILES + i + 1, :] = row_sums(k * k)
    for i in range(TILES):
        if i % (TILES // CHUNKS) == 0:
            copies[i // (TILES // CHUNKS)].wait()
        q = q_buf[i * TILE : (i + 1) * TILE, :].astype(f32)
        out_ref[i : i + 1, :] = row_sums(fold(q * q))


AT_DEST, AT_SENT, AT_PLACE, AT_STAY = DOCS, 2 * DOCS, 3 * DOCS, 4 * DOCS


def layout_kernel(
    me_ref, len_ref, dest_ref, shift_ref, q_far,
    start_ref, tile_ref, table_ref, q_near, sem,
):
    copy = pltpu.make_async_copy(q_far, q_near, sem)
    copy.start()
    rows = start_ref.shape[0]
    position = lax.broadcasted_iota(jnp.int32, (rows, TILE), 0) * TILE + lax.broadcasted_iota(
        jnp.int32, (rows, TILE), 1
    )
    zero = jnp.int32(0)
    me = me_ref[0]

    def step(j, carry):
        end, start, kept, count, lows = carry
        length = len_ref[0, j]
        stays = dest_ref[0, j] == me
        table_ref[j] = end
        table_ref[AT_DEST + j] = dest_ref[0, j]
        table_ref[AT_SENT + j] = jnp.where(stays, 0, length)
        table_ref[AT_PLACE + j] = shift_ref[0, j]
        slot = AT_STAY + jnp.where(stays, jnp.minimum(count, STAYING - 1), STAYING)
        table_ref[slot] = end
        table_ref[8 + slot] = kept
        table_ref[16 + slot] = length
        kept = jnp.where(stays, kept + length, kept)
        count = jnp.where(stays, count + 1, count)
        end = end + length
        start = jnp.where(position >= end, end, start)
        lows = tuple(jnp.where(end <= i * TILE, end, low) for i, low in enumerate(lows))
        return end, start, kept, count, lows

    _, start, _, _, lows = lax.fori_loop(
        0,
        DOCS,
        step,
        (zero, jnp.zeros((rows, TILE), jnp.int32), zero, zero, (zero,) * TILES),
        unroll=6,
    )
    start_ref[...] = start
    base = zero
    for i in range(TILES):
        need = (i + 1) * TILE - lows[i]
        size = jnp.int32(WINDOWS[0])
        for smaller, larger in zip(WINDOWS, WINDOWS[1:]):
            size = jnp.where(need > smaller, larger, size)
        tile_ref[i] = (i + 1) * TILE - size
        tile_ref[16 + i] = size
        tile_ref[32 + i] = base
        base = base + size
    copy.wait()


def window_of(tile_ref, i, size):
    return pl.ds(pl.multiple_of(tile_ref[i], 32), size), pl.ds(
        pl.multiple_of(tile_ref[32 + i], 32), size
    )


def kept_at(tile_ref, i, size, part):
    return pl.ds(pl.multiple_of(part * KEPT_ROWS + tile_ref[32 + i], 32), size)


def for_size(tile_ref, i, body):
    size_here = tile_ref[16 + i]
    for size in WINDOWS:

        @pl.when(size_here == size)
        def _(size=size):
            body(size)


def fill_slots(table_ref, lse_ref, slot_ref, home_ref, work):
    lane = lax.broadcasted_iota(jnp.int32, (8, TILE), 1)
    work[...] = jnp.zeros(work.shape, f32)
    for j in range(DOCS):
        dest = table_ref[AT_DEST + j]
        length = table_ref[AT_SENT + j]
        block = table_ref[j] >> 7
        inner = table_ref[j] & (TILE - 1)
        place = table_ref[AT_PLACE + j]
        turn = (place - inner) & (TILE - 1)
        here = pltpu.roll(lse_ref[block], turn, 1)
        after = pltpu.roll(lse_ref[block + 1], turn, 1)
        index = lane - place
        value = jnp.where(index < TILE - inner, here, after)
        work[dest] = jnp.where((index >= 0) & (index < length), value, 0.0)
    heads = [work[:, h, :] for h in range(GROUP)]
    wide = lax.broadcasted_iota(jnp.int32, (DEVICES, TILE), 1)
    gap_low = (wide >= 48) & (wide < 64)
    gap_high = wide >= 112
    last = heads[4]
    slot_ref[:, 0, :] = jnp.where(
        gap_low,
        pltpu.roll(last, 48, 1),
        jnp.where(gap_high, pltpu.roll(last, 96, 1), heads[0] + pltpu.roll(heads[1], 64, 1)),
    )
    slot_ref[:, 1, :] = jnp.where(
        gap_low, pltpu.roll(last, 16, 1), heads[2] + pltpu.roll(heads[3], 64, 1)
    )
    homes = [jnp.zeros((8, TILE), f32)] * (HOME // TILE)
    for n in range(STAYING):
        kept = table_ref[AT_STAY + 8 + n]
        length = table_ref[AT_STAY + 16 + n]
        gap = table_ref[AT_STAY + n] - kept
        block = gap >> 7
        inner = gap & (TILE - 1)
        turn = (TILE - inner) & (TILE - 1)
        moved = [pltpu.roll(lse_ref[block + b], turn, 1) for b in range(HOME // TILE + 1)]
        for b in range(HOME // TILE):
            value = jnp.where(lane < TILE - inner, moved[b], moved[b + 1])
            column = lane + b * TILE
            inside = (column >= kept) & (column < kept + length)
            homes[b] = jnp.where(inside, value, homes[b])
    home_ref[...] = jnp.concatenate(homes, axis=1)


def stacked(ref, rows):
    return jnp.concatenate([ref[rows, h * HDIM : (h + 1) * HDIM] for h in range(GROUP)], axis=0)


def scores_kernel(
    tile_ref, table_ref, start_ref, q_ref, k_ref, v_ref, g_hbm, qg_ref, kg_ref, s0_ref, s1_ref, s2_ref, s3_ref,
    recip_ref, kept_ref, dots_ref, slot_hbm, home_ref,
    dot_acc, kn_ref, lse_ref, qn_ref, g_ref, buf_ref, work, slot_ref, in_sems, qn_sems, thin_sems, sems,
):
    per_chunk = TILES // CHUNKS

    def arrival(c):
        part = pl.ds(pl.multiple_of(c * CHUNK, CHUNK), CHUNK)
        return pltpu.make_async_copy(g_hbm.at[part], g_ref.at[part], in_sems.at[c])

    for c in range(CHUNKS):
        arrival(c).start()
    total = s0_ref[...] + s1_ref[...] + s2_ref[...] + s3_ref[...]
    recip = jnp.concatenate(
        [
            lax.rsqrt(total[:TILES] * (1.0 / WIDTH_Q) + eps),
            lax.rsqrt(total[TILES:] * (1.0 / WIDTH_K) + eps),
        ],
        axis=0,
    )
    recip_ref[...] = recip
    columns = turned(recip)
    lse_ref[TILES:] = jnp.zeros((lse_ref.shape[0] - TILES, 8, TILE), f32)
    dot_acc[...] = jnp.zeros(dot_acc.shape, f32)
    for i in range(TILES):
        rows = slice(i * TILE, (i + 1) * TILE)
        col_k = columns[:, TILES + i : TILES + i + 1]
        kn_ref[rows, :] = (k_ref[rows, :].astype(f32) * col_k * kg_ref[...]).astype(bf16)

    kn_copy = pltpu.make_async_copy(kn_ref, kept_ref.at[KEYS_AT, pl.ds(0, HDIM)], thin_sems.at[0])
    kn_copy.start()

    def departure(c):
        near = pl.ds(pl.multiple_of(c * CHUNK, CHUNK), CHUNK)
        far = pl.ds(pl.multiple_of(2 * KEPT_ROWS + c * CHUNK, 32), CHUNK)
        return pltpu.make_async_copy(qn_ref.at[near], kept_ref.at[far], qn_sems.at[c])

    for i in range(TILES):
        rows = slice(i * TILE, (i + 1) * TILE)
        col_q = columns[:, i : i + 1]
        qn_ref[rows, :] = (q_ref[rows, :].astype(f32) * col_q * qg_ref[...]).astype(bf16)
        if (i + 1) % per_chunk == 0:
            departure(i // per_chunk).start()
    def copies(i, size):
        return [
            pltpu.make_async_copy(
                buf_ref.at[kept_at(tile_ref, i, size, part)],
                kept_ref.at[kept_at(tile_ref, i, size, part)],
                sems.at[part, i],
            )
            for part in range(2)
        ]

    def tile_step(i, carry):
        rows = pl.ds(pl.multiple_of(i * TILE, TILE), TILE)
        start_row = start_ref[pl.ds(i, 1), :]

        @pl.when(lax.rem(i, per_chunk) == 0)
        def _():
            arrival(lax.div(i, per_chunk)).wait()

        def body(size):
            window = pl.ds(pl.multiple_of(tile_ref[i], 32), size)
            keys = kn_ref[window, :]
            values = v_ref[window, :]
            key = tile_ref[i] + lax.broadcasted_iota(jnp.int32, (size, TILE), 0)
            query = i * TILE + lax.broadcasted_iota(jnp.int32, (size, TILE), 1)
            bias = jnp.where((key >= start_row) & (key <= query), 0.0, big_negative)
            qs = stacked(qn_ref, rows)
            gs = stacked(g_ref, rows)
            masked = mxu_nt(keys, qs) + spread(bias)
            grad_weights = mxu_nt(values, gs)
            peak = jnp.max(masked, axis=0, keepdims=True)
            grown = jnp.exp2(masked * to_exp2 - peak * to_exp2)
            mass = jnp.sum(grown, axis=0, keepdims=True)
            logs = peak * scaling + jnp.log(mass)
            inverse = 1.0 / mass
            low = (grown * inverse).astype(bf16)
            buf_ref[kept_at(tile_ref, i, size, 0), :] = low
            delta = jnp.sum(low.astype(f32) * grad_weights, axis=0, keepdims=True)
            grad = grown * (inverse * scaling) * (grad_weights - delta)
            buf_ref[kept_at(tile_ref, i, size, 1), :] = grad.astype(bf16)
            dots = fold(grad * masked)
            logs = [logs[:, h * HDIM : (h + 1) * HDIM] for h in range(GROUP)]
            logs.append(jnp.zeros((8 - GROUP, TILE), f32))
            lse_ref[pl.ds(i, 1)] = jnp.concatenate(logs, axis=0)[None]
            dots_ref[pl.ds(i, 1), :] = jnp.sum(dots, axis=0, keepdims=True)
            dot_acc[window, :] += dots
            for copy in copies(i, size):
                copy.start()

        for_size(tile_ref, i, body)
        return carry

    lax.fori_loop(0, TILES, tile_step, 0)
    fill_slots(table_ref, lse_ref, slot_ref, home_ref, work)
    slot_copy = pltpu.make_async_copy(slot_ref, slot_hbm, thin_sems.at[1])
    slot_copy.start()
    for i in range(TILES):
        dots_ref[TILES + i : TILES + i + 1, :] = row_sums(dot_acc[i * TILE : (i + 1) * TILE, :])
    kn_copy.wait()
    for c in range(CHUNKS):
        departure(c).wait()

    def drain(i, carry):
        def body(size):
            for copy in copies(i, size):
                copy.wait()

        for_size(tile_ref, i, body)
        return carry

    lax.fori_loop(0, TILES, drain, 0)
    slot_copy.wait()


def finish_kernel(
    tile_ref, kept_ref, g_hbm, q_hbm, k_hbm, qg_ref, kg_ref, recip_ref,
    s0_ref, s1_ref, s2_ref, s3_ref,
    gq_ref, gk_ref, gv_ref,
    dk_acc, dv_acc, dq_buf, gq_buf, kn_ref, qn_ref, g_ref, q_ref, k_ref, gk_buf, gv_buf, buf_ref, cube_ref,
    in_sems, thin_sems, sems, out_sems,
):
    per_chunk = TILES // CHUNKS

    def chunk_copies(c):
        part = pl.ds(pl.multiple_of(c * CHUNK, CHUNK), CHUNK)
        far = pl.ds(pl.multiple_of(2 * KEPT_ROWS + c * CHUNK, 32), CHUNK)
        return [
            pltpu.make_async_copy(kept_ref.at[far], qn_ref.at[part], in_sems.at[0, c]),
            pltpu.make_async_copy(g_hbm.at[part], g_ref.at[part], in_sems.at[1, c]),
            pltpu.make_async_copy(q_hbm.at[part], q_ref.at[part], in_sems.at[2, c]),
        ]

    def out_copy(c):
        part = pl.ds(pl.multiple_of(c * CHUNK, CHUNK), CHUNK)
        return pltpu.make_async_copy(gq_buf.at[part], gq_ref.at[part], out_sems.at[c])

    def copies(i, size):
        return [
            pltpu.make_async_copy(
                kept_ref.at[kept_at(tile_ref, i, size, part)],
                buf_ref.at[kept_at(tile_ref, i, size, part)],
                sems.at[part, i],
            )
            for part in range(2)
        ]

    kn_copy = pltpu.make_async_copy(kept_ref.at[KEYS_AT, pl.ds(0, HDIM)], kn_ref, thin_sems.at[0])
    k_copy = pltpu.make_async_copy(k_hbm, k_ref, thin_sems.at[1])
    gk_copy = pltpu.make_async_copy(gk_buf, gk_ref, thin_sems.at[2])
    gv_copy = pltpu.make_async_copy(gv_buf, gv_ref, thin_sems.at[3])
    kn_copy.start()

    def begin(i, carry):
        @pl.when(lax.rem(i, per_chunk) == 0)
        def _():
            for copy in chunk_copies(lax.div(i, per_chunk)):
                copy.start()

        def body(size):
            for copy in copies(i, size):
                copy.start()

        for_size(tile_ref, i, body)
        return carry

    lax.fori_loop(0, TILES, begin, 0)
    k_copy.start()
    dk_acc[...] = jnp.zeros(dk_acc.shape, f32)
    dv_acc[...] = jnp.zeros(dv_acc.shape, f32)
    recip = recip_ref[...]
    dots = s0_ref[...] + s1_ref[...] + s2_ref[...] + s3_ref[...]
    cube_ref[:TILES, :] = recip[:TILES] * recip[:TILES] * dots[:TILES] * (1.0 / WIDTH_Q)
    cube_ref[TILES:, :] = recip[TILES:] * recip[TILES:] * dots[TILES:] * (1.0 / WIDTH_K)
    kn_copy.wait()

    def finish_queries(i):
        rows = pl.ds(pl.multiple_of(i * TILE, TILE), TILE)
        factor = spread(column(recip_ref[pl.ds(i, 1), :])) * qg_ref[...]
        cube = spread(column(cube_ref[pl.ds(i, 1), :]))
        gq_buf[rows, :] = (
            factor * dq_buf[rows, :].astype(f32) - q_ref[rows, :].astype(f32) * cube
        ).astype(bf16)

    def tile_step(i, carry):
        rows = pl.ds(pl.multiple_of(i * TILE, TILE), TILE)

        @pl.when(lax.rem(i, per_chunk) == 0)
        def _():
            for copy in chunk_copies(lax.div(i, per_chunk)):
                copy.wait()

        def body(size):
            for copy in copies(i, size):
                copy.wait()
            finish_queries(jnp.maximum(i - 1, 0))
            window = pl.ds(pl.multiple_of(tile_ref[i], 32), size)
            weights = buf_ref[kept_at(tile_ref, i, size, 0), :]
            grads = buf_ref[kept_at(tile_ref, i, size, 1), :]
            dv_acc[window, :] += mxu_nn(weights, stacked(g_ref, rows))
            dk_acc[window, :] += mxu_nn(grads, stacked(qn_ref, rows))
            dq = mxu_tn(grads, kn_ref[window, :]).astype(bf16)
            for h in range(GROUP):
                dq_buf[rows, h * HDIM : (h + 1) * HDIM] = dq[h * TILE : (h + 1) * TILE]

        for_size(tile_ref, i, body)

        @pl.when((lax.rem(i, per_chunk) == 0) & (i > 0))
        def _():
            out_copy(lax.div(i, per_chunk) - 1).start()

        return carry

    dq_buf[:TILE, :] = jnp.zeros((TILE, GROUP * HDIM), bf16)
    lax.fori_loop(0, TILES, tile_step, 0)
    finish_queries(TILES - 1)
    out_copy(CHUNKS - 1).start()
    gv_buf[...] = dv_acc[...].astype(bf16)
    gv_copy.start()
    k_copy.wait()
    for i in range(TILES):
        rows = slice(i * TILE, (i + 1) * TILE)
        at = slice(TILES + i, TILES + i + 1)
        scaled = dk_acc[rows, :].astype(bf16).astype(f32) * kg_ref[...]
        gk_buf[rows, :] = (
            column(recip_ref[at, :]) * scaled - k_ref[rows, :].astype(f32) * column(cube_ref[at, :])
        ).astype(bf16)
    gk_copy.start()
    for c in range(CHUNKS):
        out_copy(c).wait()
    gv_copy.wait()
    gk_copy.wait()


def assemble_kernel(got_ref, home_ref, out_ref, work):
    out_ref[:, :HOME] = home_ref[:GROUP, :]
    upper, lower = got_ref[:, 0, :], got_ref[:, 1, :]
    wide = lax.broadcasted_iota(jnp.int32, (DEVICES, TILE), 1)
    work[:, 0, :] = upper
    work[:, 1, :] = pltpu.roll(upper, 64, 1)
    work[:, 2, :] = lower
    work[:, 3, :] = pltpu.roll(lower, 64, 1)
    work[:, 4, :] = jnp.where(
        wide < 16,
        pltpu.roll(upper, TILE - 48, 1),
        jnp.where(wide < 32, pltpu.roll(upper, TILE - 96, 1), pltpu.roll(lower, TILE - 16, 1)),
    )
    lane = lax.broadcasted_iota(jnp.int32, (8, TILE), 1)
    blocks = [None] * (DEVICES * SLOT // TILE)
    for s in range(DEVICES):
        block, place = divmod(s * SLOT, TILE)
        value = work[s]
        value = pltpu.roll(value, place, 1) if place else value
        if blocks[block] is None:
            blocks[block] = value
        else:
            blocks[block] = jnp.where(lane >= place, value, blocks[block])
        if place + SLOT > TILE:
            blocks[block + 1] = value
    for b, value in enumerate(blocks):
        out_ref[:, HOME + b * TILE : HOME + (b + 1) * TILE] = value[:GROUP]


def from_others(values):
    size = lax.axis_size("head")
    return [values] + [
        lax.ppermute(values, "head", [(i, (i + s) % size) for i in range(size)])
        for s in range(1, size)
    ]


def local(q_raw, k_raw, v_proj, d_out, q_gain, k_gain, doc_lengths, plan_dest, plan_offset):
    me = lax.axis_index("dp").astype(jnp.int32).reshape(1)
    qg = q_gain.reshape(1, -1)
    kg = k_gain.reshape(1, -1)
    stat = ((2 * TILES, TILE), f32)
    wide = ((SEQ, GROUP * HDIM), bf16)
    thin = ((SEQ, HDIM), bf16)
    kept = ((FAR_ROWS, GROUP * HDIM), bf16)

    (squares,) = call(
        square_kernel,
        [stat],
        [HBM] * 2,
        scratch=[pltpu.VMEM(*wide), pltpu.VMEM(*thin), pltpu.SemaphoreType.DMA((CHUNKS + 1,))],
        vmem=53.7,
        name="squares",
    )(q_raw, k_raw)
    start, tiles, table, q_near = call(
        layout_kernel,
        [
            ((16, TILE), jnp.int32),
            ((48,), jnp.int32),
            ((AT_STAY + 24,), jnp.int32),
            wide,
        ],
        [SMEM] * 4 + [HBM],
        [VMEM] + [SMEM] * 2 + [HBM],
        scratch=[pltpu.SemaphoreType.DMA],
        vmem=50.5,
        name="layout",
    )(me, doc_lengths, plan_dest, plan_offset, q_raw)
    recip, kept, dots, slots, home = call(
        scores_kernel,
        [stat, kept, stat, ((DEVICES, 2, TILE), f32), ((8, HOME), f32)],
        [SMEM] * 2 + [VMEM] * 4 + [HBM] + [VMEM] * 6,
        out_specs=[VMEM, HBM, VMEM, HBM, VMEM],
        scratch=[
            pltpu.VMEM((SEQ, HDIM), f32),
            pltpu.VMEM(*thin),
            pltpu.VMEM((16, 8, TILE), f32),
            pltpu.VMEM(*wide),
            pltpu.VMEM(*wide),
            pltpu.VMEM((2 * KEPT_ROWS, GROUP * HDIM), bf16),
            pltpu.VMEM((DEVICES, 8, TILE), f32),
            pltpu.VMEM((DEVICES, 2, TILE), f32),
            pltpu.SemaphoreType.DMA((CHUNKS,)),
            pltpu.SemaphoreType.DMA((CHUNKS,)),
            pltpu.SemaphoreType.DMA((2,)),
            pltpu.SemaphoreType.DMA((2, TILES)),
        ],
        flops=10**9,
        vmem=50.5,
        name="scores",
    )(tiles, table, start, q_near, k_raw, v_proj, d_out, qg, kg, *from_others(squares))
    all_dots = from_others(dots)
    got = lax.all_to_all(slots, "dp", split_axis=0, concat_axis=0, tiled=True)
    grad_q, grad_k, grad_v = call(
        finish_kernel,
        [wide, thin, thin],
        [SMEM] + [HBM] * 4 + [VMEM] * 7,
        out_specs=[HBM] * 3,
        scratch=[
            pltpu.VMEM((SEQ, HDIM), f32),
            pltpu.VMEM((SEQ, HDIM), f32),
            pltpu.VMEM(*wide),
            pltpu.VMEM(*wide),
            pltpu.VMEM(*thin),
            pltpu.VMEM(*wide),
            pltpu.VMEM(*wide),
            pltpu.VMEM(*wide),
            pltpu.VMEM(*thin),
            pltpu.VMEM(*thin),
            pltpu.VMEM(*thin),
            pltpu.VMEM((2 * KEPT_ROWS, GROUP * HDIM), bf16),
            pltpu.VMEM((2 * TILES, TILE), f32),
            pltpu.SemaphoreType.DMA((3, CHUNKS)),
            pltpu.SemaphoreType.DMA((4,)),
            pltpu.SemaphoreType.DMA((2, TILES)),
            pltpu.SemaphoreType.DMA((CHUNKS,)),
        ],
        flops=10**10,
        vmem=53.7,
        name="finish",
    )(tiles, kept, d_out, q_raw, k_raw, qg, kg, recip, *all_dots)
    (balanced,) = call(
        assemble_kernel,
        [((GROUP, HOME + DEVICES * SLOT), f32)],
        [VMEM] * 2,
        scratch=[pltpu.VMEM((DEVICES, 8, TILE), f32)],
        name="assemble",
    )(got, home)
    return grad_q, grad_k, grad_v, balanced


def solution(mesh):
    in_specs = (
        P("dp", "head"),
        P("dp", "head"),
        P("dp", "head"),
        P("dp", "head"),
        P("head"),
        P("head"),
        P("dp", None),
        P("dp", None),
        P("dp", None),
    )
    out_specs = (P("dp", "head"), P("dp", "head"), P("dp", "head"), P("head", "dp"))
    return jax.shard_map(local, mesh=mesh, in_specs=in_specs, out_specs=out_specs, check_vma=False)
```
